32 devices in a mesh: batch: 2 (over core), seq: 16 (over z, y, x).
Axes of the slice: x: 2, y: 2, z: 4, core: 2. Of those that a mesh axis runs over, the one named last changes fastest.
Arguments:
- inputs: bfloat16 [4, 8192, 1024], P('batch', 'seq'), may hold values from -6 to 6
- doc_ids: int32 [4, 8192], P('batch', 'seq'), may hold values from 0 to 1, as said below
- w_query: bfloat16 [1024, 1024], replicated, may hold values from -0.1875 to 0.1875
- w_key: bfloat16 [1024, 1024], replicated, may hold values from -0.1875 to 0.1875
- w_value: bfloat16 [1024, 1024], replicated, may hold values from -0.1875 to 0.1875
- w_outgate: bfloat16 [1024, 1024], replicated, may hold values from -0.1875 to 0.1875
- w_output: bfloat16 [1024, 1024], replicated, may hold values from -0.375 to 0.375
- w_gate: bfloat16 [1024, 2816], replicated, may hold values from -0.1875 to 0.1875
- w_up: bfloat16 [1024, 2816], replicated, may hold values from -0.1875 to 0.1875
- w_down: bfloat16 [2816, 1024], replicated, may hold values from -0.109375 to 0.109375
- head_gain: float32 [1024], replicated, may hold values from 0.1 to 1.9
- cotangent: bfloat16 [4, 8192, 1024], P('batch', 'seq'), may hold values from -6 to 6
Outputs:
- block_out: bfloat16 [4, 8192, 1024], P('batch', 'seq')
- input_grad: bfloat16 [4, 8192, 1024], P('batch', 'seq')
- grad_query: float32 [1024, 1024], P(('batch', 'seq'))
- grad_key: float32 [1024, 1024], P(('batch', 'seq'))
- grad_value: float32 [1024, 1024], P(('batch', 'seq'))
- grad_outgate: float32 [1024, 1024], P(('batch', 'seq'))
- grad_output: float32 [1024, 1024], P(('batch', 'seq'))
- grad_gate: float32 [1024, 2816], P(('batch', 'seq'))
- grad_up: float32 [1024, 2816], P(('batch', 'seq'))
- grad_down: float32 [2816, 1024], P(('batch', 'seq'))
- grad_gain: float32 [1024], P(('batch', 'seq'))
The draws below stay inside these ranges and needn't reach their ends.
Inputs may be any that keep to these rules, and one draw needn't show every extreme that they name: `doc_ids`: within each row the ids start at 0, never fall, and rise by one at the first token of each new document.
All inputs are finite; a program needn't handle non-finite values.
Results may differ from the reference program's by a relative error of at most 0.014.
Values sent between devices are 32-bit elements; how exact they have to be, the bound alone decides.
No kernel may reach another device: no remote copies, remote signals or barrier semaphores. Data moves between devices by JAX's collectives and lax.ppermute only.
A program may use at most 320 MiB of HBM per device.

```python
import jax
import jax.numpy as jnp
from jax import lax

D = 1024
HEADS = 16
HEAD_DIM = 64
FF = 2816
ROWS_DEV = 2
BLOCK = 512
DOC = 2048
ROWS = 4
LEN = 8192


def draw_doc_ids(key, part):
    key = jax.random.fold_in(key, 11)
    key_lengths, key_span, key_pick = jax.random.split(key, 3)
    slot_count = LEN // (DOC // 2) + 2
    lengths = jax.random.randint(key_lengths, (ROWS, slot_count), DOC // 2, 2 * DOC, dtype=jnp.int32)
    boundary = jnp.cumsum(lengths, axis=1, dtype=jnp.int32)
    places = jnp.arange(LEN, dtype=jnp.int32)
    packed = jnp.sum((boundary[:, None, :] <= places[None, :, None]).astype(jnp.int32), axis=-1, dtype=jnp.int32)
    packed = jnp.minimum(packed, jnp.int32((LEN - 1) // (2 * DOC)))
    span_end = jnp.int32(LEN) - jax.random.randint(key_span, (ROWS,), 1, BLOCK, dtype=jnp.int32)
    spanning = (places[None, :] >= span_end[:, None]).astype(jnp.int32)
    chosen_row = jax.random.randint(key_pick, (ROWS // ROWS_DEV,), 0, ROWS_DEV, dtype=jnp.int32)
    row_index = jnp.arange(ROWS, dtype=jnp.int32)
    chosen = row_index % ROWS_DEV == jnp.repeat(chosen_row, ROWS_DEV)
    return jnp.where(chosen[:, None], spanning, packed).astype(jnp.int32)


def levels(rng, extent, shards, smallest, high):
    factor_of = 1.0
    for axis_at, parts in shards:
        heights = jax.random.uniform(jax.random.fold_in(jax.random.fold_in(rng, 6), axis_at), (parts,), jnp.float32, smallest / len(shards), high / len(shards))
        factor_of = factor_of * jnp.repeat(jnp.exp(heights), extent[axis_at] // parts).reshape((-1,) + (1,) * (len(extent) - 1 - axis_at))
    return factor_of


def gaussian(own_key, shape, scale, bound, shards=(), held_as=jnp.bfloat16):
    gain = levels(own_key, shape, shards, -0.22, 0.18) if shards else 1.0
    drawn = jax.random.normal(own_key, shape, jnp.float32) * scale * gain
    return jnp.minimum(jnp.maximum(drawn, -bound), bound).astype(held_as)


def setup_inputs(seed: int = 0) -> dict:
    streams_of = jax.random.split(jax.random.key(seed), 13)
    return {
        "inputs": gaussian(streams_of[0], (ROWS, LEN, D), 1.0, 6.0, ((0, 2), (1, 16))),
        "doc_ids": draw_doc_ids(jax.random.fold_in(streams_of[12], 71), 0),
        "w_query": gaussian(streams_of[2], (D, D), D ** -0.5, 0.1875),
        "w_key": gaussian(streams_of[3], (D, D), D ** -0.5, 0.1875),
        "w_value": gaussian(streams_of[4], (D, D), D ** -0.5, 0.1875),
        "w_outgate": gaussian(streams_of[5], (D, D), D ** -0.5, 0.1875),
        "w_output": gaussian(streams_of[6], (D, D), (D // 4) ** -0.5, 0.375),
        "w_gate": gaussian(streams_of[7], (D, FF), D ** -0.5, 0.1875),
        "w_up": gaussian(streams_of[8], (D, FF), D ** -0.5, 0.1875),
        "w_down": gaussian(streams_of[9], (FF, D), FF ** -0.5, 0.109375),
        "head_gain": jnp.clip(1.0 + 0.18 * jax.random.normal(streams_of[10], (D,), jnp.float32), 0.1, 1.9),
        "cotangent": gaussian(streams_of[11], (ROWS, LEN, D), 1.0, 6.0, ((0, 2), (1, 16))),
    }


epsilon = 1e-06

@jax.custom_vjp
def low(v):
    return lax.optimization_barrier(v.astype(jnp.bfloat16)).astype(jnp.float32)

@jax.custom_vjp
def low_back(v):
    return v

def low_keep(v):
    return (low(v), None)

def low_pass(kept, grad):
    return (grad,)

def back_keep(v):
    return (v, None)

def back_low(kept, grad):
    return (low(grad),)
low.defvjp(low_keep, low_pass)
low_back.defvjp(back_keep, back_low)

def matmul(first_op, second_op):
    return jnp.dot(first_op, second_op, precision=lax.Precision.HIGHEST, preferred_element_type=jnp.float32)

def normalize(values):
    return values * lax.rsqrt(lax.optimization_barrier(jnp.mean(values * values, axis=-1, keepdims=True)) + epsilon)

def block_step(state_pair, pieces):
    state_sum, state_id = state_pair
    qry_block, key_block, val_block, id_block = pieces
    id_block = id_block.astype(jnp.int32)
    places = jnp.arange(id_block.shape[0], dtype=jnp.int32)
    causal = places[:, None] >= places[None, :]
    allowed = causal & (id_block[:, None] == id_block[None, :])
    raw_scores = jnp.einsum('thd,shd->hts', qry_block, key_block, precision=lax.Precision.HIGHEST)
    scores = low(low_back(jnp.where(allowed[None], raw_scores, jnp.zeros_like(raw_scores))))
    inside = jnp.einsum('hts,shd->thd', scores, val_block, precision=lax.Precision.HIGHEST)
    carried = low(state_sum)
    across = jnp.einsum('thd,hde->the', qry_block, carried, precision=lax.Precision.HIGHEST)
    matched = id_block == state_id
    result = inside + jnp.where(matched[:, None, None], across, jnp.zeros_like(across))
    last_id = id_block[-1].astype(jnp.int32)
    in_last = (id_block == last_id).astype(key_block.dtype)
    contrib = low_back(jnp.einsum('thd,the->hde', key_block * in_last[:, None, None], val_block, precision=lax.Precision.HIGHEST))
    new_state = (jnp.where(state_id == last_id, state_sum, jnp.zeros_like(state_sum)) + contrib).astype(state_sum.dtype)
    return ((new_state, last_id), result)

def attention(queries, key_heads, val_heads, doc_row):
    length = queries.shape[0]
    num_blocks = length // BLOCK
    block_shape = (num_blocks, BLOCK, HEADS, HEAD_DIM)
    initial = (jnp.zeros((HEADS, HEAD_DIM, HEAD_DIM), queries.dtype), jnp.array(-1, dtype=jnp.int32))
    last_carry, outputs = lax.scan(jax.checkpoint(block_step), initial, (queries.reshape(block_shape), key_heads.reshape(block_shape), val_heads.reshape(block_shape), doc_row.astype(jnp.int32).reshape(num_blocks, BLOCK)))
    return outputs.reshape(length, HEADS * HEAD_DIM)

def forward(inputs, doc_row, w_query, w_key, w_value, w_outgate, w_output, w_gate, w_up, w_down, head_gain):
    length = inputs.shape[0]
    normed_in = low(normalize(inputs))
    queries = low(jax.nn.softplus(low_back(matmul(normed_in, w_query))))
    key_heads = low(jax.nn.softplus(low_back(matmul(normed_in, w_key))))
    val_heads = low(low_back(matmul(normed_in, w_value)))
    out_gate = jax.nn.sigmoid(low_back(matmul(normed_in, w_outgate)))
    mixed_heads = low_back(attention(queries, key_heads, val_heads, doc_row))
    unit_heads = normalize(mixed_heads.reshape(length, HEADS, HEAD_DIM)).reshape(length, HEADS * HEAD_DIM)
    gated_out = low(unit_heads * head_gain * out_gate)
    hidden_sum = inputs + low_back(matmul(gated_out, w_output))
    normed_mid = low(normalize(hidden_sum))
    gate_pre = low_back(matmul(normed_mid, w_gate))
    up_pre = low_back(matmul(normed_mid, w_up))
    product = low(gate_pre * up_pre)
    return hidden_sum + low_back(matmul(product, w_down))

def reference(inputs, doc_ids, w_query, w_key, w_value, w_outgate, w_output, w_gate, w_up, w_down, head_gain, cotangent):
    params = tuple((weight.astype(jnp.float32) for weight in (w_query, w_key, w_value, w_outgate, w_output, w_gate, w_up, w_down, head_gain)))

    def one_row(totals, row_data):
        row_in, row_ids, row_cot = row_data

        def local_fn(values, *weights):
            return forward(values, row_ids, *weights)
        row_out, pullback = jax.vjp(local_fn, row_in.astype(jnp.float32), *params)
        gradients = pullback(row_cot.astype(jnp.float32))
        totals = tuple(((running + gradient).astype(running.dtype) for running, gradient in zip(totals, gradients[1:])))
        return (totals, (row_out.astype(jnp.bfloat16), gradients[0].astype(jnp.bfloat16)))
    zero_totals = tuple((jnp.zeros_like(weight) for weight in params))
    totals, (outputs, input_grads) = lax.scan(one_row, zero_totals, (inputs, doc_ids.astype(jnp.int32), cotangent))
    return (outputs, input_grads, totals[0], totals[1], totals[2], totals[3], totals[4], totals[5], totals[6], totals[7], totals[8])
```

```python
import jax
import jax.numpy as jnp
from jax import lax
from jax.sharding import PartitionSpec as P

HEADS = 16
HEAD_DIM = 64


epsilon = 1e-06


def chip_grid(count):
    bits = count.bit_length() - 1
    z_bits = min(bits, 2)
    y_bits = (bits - z_bits + 1) // 2
    return z_bits, y_bits, bits - z_bits - y_bits


def seq_bit(position, bits, place):
    return (position >> (bits - 1 - place)) & 1


def piece(array, axes, picks):
    starts = [picks.get(a, 0) for a in axes] + [0] * (array.ndim - len(axes))
    sizes = [1 if a in picks else 2 for a in axes] + list(array.shape[len(axes):])
    taken = lax.dynamic_slice(array, starts, sizes)
    left = tuple(a for a in axes if a not in picks)
    return taken.reshape((2,) * len(left) + array.shape[len(axes):])


def scatter_sum(grad, order):
    count = lax.axis_size("seq")
    bits = count.bit_length() - 1
    axes = ("batch",) + tuple(range(bits))
    rows = grad.shape[0] // (2 * count)
    position = lax.axis_index("seq")
    mine = {"batch": lax.axis_index("batch")}
    for place in range(bits):
        mine[place] = seq_bit(position, bits, place)
    parts = [(grad.reshape((2,) * len(axes) + (rows,) + grad.shape[1:]), axes)]
    done = {}
    for axis in order:
        away = dict(done)
        away[axis] = 1 - mine[axis]
        outgoing = sum_pieces(parts, away)
        if axis == "batch":
            incoming = lax.ppermute(outgoing, "batch", [(0, 1), (1, 0)])
        else:
            flip = 1 << (bits - 1 - axis)
            incoming = lax.ppermute(outgoing, "seq", [(i, i ^ flip) for i in range(count)])
        done[axis] = mine[axis]
        parts.append((incoming, tuple(a for a in axes if a not in done)))
    return sum_pieces(parts, done)


def sum_pieces(parts, picks):
    total = None
    for array, axes in parts:
        one = piece(array, axes, {a: v for a, v in picks.items() if a in axes})
        total = one if total is None else total + one
    return total


def orders(count):
    z_bits, y_bits, x_bits = chip_grid(count)
    z_axes = list(range(z_bits))[::-1]
    y_axes = list(range(z_bits, z_bits + y_bits))[::-1]
    x_axes = list(range(z_bits + y_bits, z_bits + y_bits + x_bits))[::-1]
    return (
        ["batch"] + x_axes + y_axes + z_axes,
        ["batch"] + y_axes + x_axes + z_axes,
        ["batch"] + z_axes + x_axes + y_axes,
    )


def gather_ids(ids):
    count = lax.axis_size("seq")
    bits = count.bit_length() - 1
    position = lax.axis_index("seq")
    held = ids[None]
    for step in range(bits):
        flip = 1 << step
        other = lax.ppermute(held, "seq", [(i, i ^ flip) for i in range(count)])
        low = (position & flip) == 0
        held = jnp.concatenate([jnp.where(low, held, other), jnp.where(low, other, held)], axis=0)
    return held


def prefix(state, ids, reverse):
    count = lax.axis_size("seq")
    position = lax.axis_index("seq")
    z_bits, y_bits, x_bits = chip_grid(count)
    planes = 1 << z_bits
    plane = 1 << (y_bits + x_bits)
    row_count, heads = state.shape[:2]
    share = heads // plane
    z_at, at = position // plane, position % plane
    shape = (row_count, plane, share) + state.shape[2:]
    cut = state.reshape(shape)

    def pairs(k):
        return [(i, (i // plane) * plane + ((i % plane) ^ k)) for i in range(count)]

    def take(array, index):
        return lax.dynamic_index_in_dim(array, index, 1, False)

    swapped = [take(cut, at)]
    for k in range(1, plane):
        swapped.append(lax.ppermute(take(cut, at ^ k), "seq", pairs(k)))
    ids_plane = lax.dynamic_slice_in_dim(ids, z_at * plane, plane, 0)
    end = 0 if reverse else plane - 1

    def masked(flag, array):
        return jnp.where(flag[:, None, None, None], array, 0.0)

    def id_of(index):
        return lax.dynamic_index_in_dim(ids, jnp.clip(index, 0, count - 1), 0, False)

    total = None
    for k in range(plane):
        one = masked(lax.dynamic_index_in_dim(ids_plane, at ^ k, 0, False) == ids_plane[end], swapped[k])
        total = one if total is None else total + one
    passed = []
    for step in range(1, planes):
        shift = -step * plane if reverse else step * plane
        moves = [(i, i + shift) for i in range(count) if 0 <= i + shift < count]
        source = z_at + step if reverse else z_at - step
        passed.append((lax.ppermute(total, "seq", moves), source))
    results = []
    for k in range(plane):
        target_at = at ^ k
        target = z_at * plane + target_at
        near = target + 1 if reverse else target - 1
        near_id = id_of(near)
        summed = jnp.zeros_like(total)
        for j in range(plane):
            source_at = at ^ j
            before = source_at > target_at if reverse else source_at < target_at
            same = lax.dynamic_index_in_dim(ids_plane, source_at, 0, False) == near_id
            summed = summed + masked(before & same, swapped[j])
        for array, source in passed:
            there = (source < planes) if reverse else (source >= 0)
            same = id_of(source * plane + end) == near_id
            summed = summed + masked(there & same, array)
        results.append(summed)
    back = [results[0]]
    for k in range(1, plane):
        back.append(lax.ppermute(results[k], "seq", pairs(k)))
    stacked = jnp.stack(back, axis=0)
    ordered = [lax.dynamic_index_in_dim(stacked, at ^ j, 0, False) for j in range(plane)]
    carried = jnp.stack(ordered, axis=1).reshape(state.shape)
    near = position + 1 if reverse else position - 1
    exists = (near < count) & (near >= 0)
    carried = carried * exists.astype(carried.dtype)
    return carried, jnp.where(exists, id_of(near), -1.0)


def project(activations, weight):
    return jnp.dot(activations, weight, preferred_element_type=jnp.float32)


def outer_sum(activations, grads_in):
    return lax.dot_general(
        activations, grads_in, (((0,), (0,)), ((), ())), preferred_element_type=jnp.float32
    )


def project_back(grads_in, weight):
    return lax.dot_general(
        grads_in, weight, (((1,), (1,)), ((), ())), preferred_element_type=jnp.float32
    )


def rms_scale(values):
    return lax.rsqrt(jnp.mean(values * values, axis=-1, keepdims=True) + epsilon)


def norm_back(unit_vals, scale_vals, grad_vals):
    return scale_vals * (
        grad_vals - unit_vals * jnp.mean(grad_vals * unit_vals, axis=-1, keepdims=True)
    )


def softplus_grad(values):
    return jax.nn.sigmoid(values)


def local(
    inputs,
    doc_ids,
    w_query,
    w_key,
    w_value,
    w_outgate,
    w_output,
    w_gate,
    w_up,
    w_down,
    head_gain,
    cotangent,
):
    row_count, block_len, feat_width = inputs.shape
    token_count = row_count * block_len
    heads_shape = (row_count, block_len, HEADS, HEAD_DIM)
    in_flat = inputs.reshape(token_count, feat_width).astype(jnp.float32)
    scale_in = rms_scale(in_flat)
    unit_in = in_flat * scale_in
    normed_in = unit_in.astype(jnp.bfloat16)
    pre_query = project(normed_in, w_query)
    pre_key = project(normed_in, w_key)
    pre_value = project(normed_in, w_value)
    pre_outgate = project(normed_in, w_outgate)
    queries = jax.nn.softplus(pre_query).astype(jnp.bfloat16).reshape(heads_shape)
    key_heads = jax.nn.softplus(pre_key).astype(jnp.bfloat16).reshape(heads_shape)
    val_heads = pre_value.astype(jnp.bfloat16).reshape(heads_shape)
    out_gate = jax.nn.sigmoid(pre_outgate)
    ids_float = doc_ids.astype(jnp.float32)
    places = jnp.arange(block_len, dtype=jnp.int32)
    allowed = (places[:, None] >= places[None, :])[None] & (
        doc_ids[:, :, None] == doc_ids[:, None, :]
    )

    def block_scores():
        raw_scores = jnp.einsum(
            "rthd,rshd->rhts", queries, key_heads, preferred_element_type=jnp.float32
        )
        return jnp.where(allowed[:, None], raw_scores, 0.0).astype(jnp.bfloat16)

    last_ids = ids_float[:, -1]
    first_ids = ids_float[:, 0]
    in_last = (ids_float == last_ids[:, None]).astype(jnp.bfloat16)
    local_state = jnp.einsum(
        "rthd,rthe->rhde",
        key_heads * in_last[:, :, None, None],
        val_heads,
        preferred_element_type=jnp.float32,
    )
    edge_ids = gather_ids(jnp.concatenate([first_ids, last_ids]))
    carried, carried_id = prefix(local_state, edge_ids[:, row_count:], False)
    matched = (ids_float == carried_id[:, None])[:, :, None, None]
    carried_low = carried.astype(jnp.bfloat16)
    attn_probs = block_scores()
    attended = jnp.einsum(
        "rhts,rshd->rthd", attn_probs, val_heads, preferred_element_type=jnp.float32
    )
    attended = attended + jnp.where(
        matched,
        jnp.einsum("rthd,rhde->rthe", queries, carried_low, preferred_element_type=jnp.float32),
        0.0,
    )
    head_scale = rms_scale(attended)
    unit_heads = (attended * head_scale).reshape(token_count, feat_width)
    normed_heads = unit_heads * head_gain
    gated_out = (normed_heads * out_gate).astype(jnp.bfloat16)
    hidden_sum = in_flat + project(gated_out, w_output)
    scale_mid = rms_scale(hidden_sum)
    unit_mid = hidden_sum * scale_mid
    normed_mid = unit_mid.astype(jnp.bfloat16)
    gate_pre = project(normed_mid, w_gate)
    up_pre = project(normed_mid, w_up)
    product = (gate_pre * up_pre).astype(jnp.bfloat16)
    out_flat = hidden_sum + project(product, w_down)
    block_out = out_flat.astype(jnp.bfloat16).reshape(inputs.shape)
    cot_flat = cotangent.reshape(token_count, feat_width)
    cot_float = cot_flat.astype(jnp.float32)
    grad_down = outer_sum(product, cot_flat)
    back_product = project_back(cot_flat, w_down)
    back_gate = (back_product * up_pre).astype(jnp.bfloat16)
    back_up = (back_product * gate_pre).astype(jnp.bfloat16)
    grad_gate = outer_sum(normed_mid, back_gate)
    grad_up = outer_sum(normed_mid, back_up)
    back_mid = project_back(back_gate, w_gate) + project_back(back_up, w_up)
    back_hidden = cot_float + norm_back(unit_mid, scale_mid, back_mid)
    back_branch = back_hidden.astype(jnp.bfloat16)
    grad_output = outer_sum(gated_out, back_branch)
    back_gated = project_back(back_branch, w_output)
    back_outgate = (back_gated * normed_heads * out_gate * (1.0 - out_gate)).astype(jnp.bfloat16)
    back_normed = back_gated * out_gate
    grad_gain = jnp.sum(unit_heads * back_normed, axis=0)
    back_unit = (back_normed * head_gain).reshape(heads_shape)
    back_attended = norm_back(unit_heads.reshape(heads_shape), head_scale, back_unit).astype(
        jnp.bfloat16
    )
    in_first = (ids_float == first_ids[:, None]).astype(jnp.bfloat16)
    local_grad = jnp.einsum(
        "rthd,rthe->rhde",
        queries * in_first[:, :, None, None],
        back_attended,
        preferred_element_type=jnp.float32,
    )
    grad_in, grad_id = prefix(local_grad, edge_ids[:, :row_count], True)
    attn_probs = block_scores()
    back_scores = jnp.where(
        allowed[:, None],
        jnp.einsum("rthd,rshd->rhts", back_attended, val_heads, preferred_element_type=jnp.float32),
        0.0,
    ).astype(jnp.bfloat16)
    grad_low = grad_in.astype(jnp.bfloat16)
    uses_grad = (ids_float == grad_id[:, None])[:, :, None, None]
    back_queries = jnp.einsum(
        "rhts,rshd->rthd", back_scores, key_heads, preferred_element_type=jnp.float32
    )
    back_queries = back_queries + jnp.where(
        matched,
        jnp.einsum(
            "rthe,rhde->rthd", back_attended, carried_low, preferred_element_type=jnp.float32
        ),
        0.0,
    )
    back_keys = jnp.einsum(
        "rhts,rthd->rshd", back_scores, queries, preferred_element_type=jnp.float32
    )
    back_keys = back_keys + jnp.where(
        uses_grad,
        jnp.einsum("rthe,rhde->rthd", val_heads, grad_low, preferred_element_type=jnp.float32),
        0.0,
    )
    back_values = jnp.einsum(
        "rhts,rthd->rshd", attn_probs, back_attended, preferred_element_type=jnp.float32
    )
    back_values = back_values + jnp.where(
        uses_grad,
        jnp.einsum("rthd,rhde->rthe", key_heads, grad_low, preferred_element_type=jnp.float32),
        0.0,
    )
    back_query = (back_queries.reshape(token_count, feat_width) * softplus_grad(pre_query)).astype(
        jnp.bfloat16
    )
    back_key = (back_keys.reshape(token_count, feat_width) * softplus_grad(pre_key)).astype(
        jnp.bfloat16
    )
    back_value = back_values.reshape(token_count, feat_width).astype(jnp.bfloat16)
    grad_query = outer_sum(normed_in, back_query)
    grad_key = outer_sum(normed_in, back_key)
    grad_value = outer_sum(normed_in, back_value)
    grad_outgate = outer_sum(normed_in, back_outgate)
    back_in = project_back(back_query, w_query) + project_back(back_key, w_key)
    back_in = back_in + project_back(back_value, w_value) + project_back(back_outgate, w_outgate)
    input_grad = (
        (back_hidden + norm_back(unit_in, scale_in, back_in))
        .astype(jnp.bfloat16)
        .reshape(inputs.shape)
    )
    x_first, y_first, z_first = orders(lax.axis_size("seq"))
    all_shards = (
        scatter_sum(grad_query, z_first),
        scatter_sum(grad_key, x_first),
        scatter_sum(grad_value, y_first),
        scatter_sum(grad_outgate, z_first),
        scatter_sum(grad_output, z_first),
        scatter_sum(grad_gate, y_first),
        scatter_sum(grad_up, x_first),
        scatter_sum(grad_down, x_first),
        scatter_sum(grad_gain, x_first),
    )
    return (block_out, input_grad) + all_shards


def solution(mesh):
    return jax.shard_map(
        local,
        mesh=mesh,
        in_specs=(
            P("batch", "seq", None),
            P("batch", "seq"),
            P(),
            P(),
            P(),
            P(),
            P(),
            P(),
            P(),
            P(),
            P(),
            P("batch", "seq", None),
        ),
        out_specs=(
            P("batch", "seq", None),
            P("batch", "seq", None),
            P(("batch", "seq"), None),
            P(("batch", "seq"), None),
            P(("batch", "seq"), None),
            P(("batch", "seq"), None),
            P(("batch", "seq"), None),
            P(("batch", "seq"), None),
            P(("batch", "seq"), None),
            P(("batch", "seq"), None),
            P(("batch", "seq")),
        ),
        check_vma=False,
    )
```

```python
import functools

import jax
import jax.numpy as jnp
from jax import lax
from jax.experimental import pallas as pl
from jax.experimental.pallas import tpu as pltpu
from jax.sharding import PartitionSpec as P

HEADS = 16
HEAD_DIM = 64
GROUP = 4 * HEAD_DIM
TILE = 256
EPSILON = 1e-06
F32 = jnp.float32
BF16 = jnp.bfloat16
VMEM_BYTES = 56 << 20


def chip_grid(count):
    bits = count.bit_length() - 1
    z_bits = min(bits, 2)
    y_bits = (bits - z_bits + 1) // 2
    return z_bits, y_bits, bits - z_bits - y_bits


def orders(count):
    z_bits, y_bits, x_bits = chip_grid(count)
    z_axes = list(range(z_bits))[::-1]
    y_axes = list(range(z_bits, z_bits + y_bits))[::-1]
    x_axes = list(range(z_bits + y_bits, z_bits + y_bits + x_bits))[::-1]
    return x_axes + y_axes + z_axes, y_axes + x_axes + z_axes, z_axes + x_axes + y_axes


def piece(array, axes, picks, columns):
    held = len(axes)
    starts = [picks.get(a, 0) for a in axes] + [0] * (array.ndim - held)
    sizes = [1 if a in picks else 2 for a in axes] + list(array.shape[held:])
    if columns is not None:
        starts[-1] = columns[0]
        sizes[-1] = columns[1] - columns[0]
    taken = lax.dynamic_slice(array, starts, sizes)
    left = sum(a not in picks for a in axes)
    return taken.reshape((2,) * left + tuple(sizes[held:]))


def sum_pieces(parts, picks):
    total = None
    for array, axes, columns in parts:
        one = piece(array, axes, {a: v for a, v in picks.items() if a in axes}, columns)
        total = one if total is None else total + one
    return total


def scatter_seq(halves, order, columns=None):
    count = lax.axis_size("seq")
    bits = count.bit_length() - 1
    axes = tuple(range(bits))
    position = lax.axis_index("seq")
    mine = {a: (position >> (bits - 1 - a)) & 1 for a in axes}
    rows = halves[0].shape[0] // count
    parts = [(h.reshape((2,) * bits + (rows,) + h.shape[1:]), axes, columns) for h in halves]
    done = {}
    for axis in order:
        outgoing = sum_pieces(parts, {**done, axis: 1 - mine[axis]})
        flip = 1 << (bits - 1 - axis)
        incoming = lax.ppermute(outgoing, "seq", [(i, i ^ flip) for i in range(count)])
        done[axis] = mine[axis]
        parts.append((incoming, tuple(a for a in axes if a not in done), None))
    return sum_pieces(parts, done)


def to_core(array):
    return lax.ppermute(array, "batch", [(0, 1), (1, 0)])


def call(kernel, grid, in_specs, out_specs, out_shape, scratch=(), prefetch=0, flops=0, bytes_accessed=0):
    spec = pltpu.PrefetchScalarGridSpec(
        num_scalar_prefetch=prefetch,
        grid=grid,
        in_specs=in_specs,
        out_specs=out_specs,
        scratch_shapes=scratch,
    )
    return pl.pallas_call(
        kernel,
        grid_spec=spec,
        out_shape=out_shape,
        compiler_params=pltpu.CompilerParams(vmem_limit_bytes=VMEM_BYTES),
        cost_estimate=pl.CostEstimate(flops=flops, bytes_accessed=bytes_accessed, transcendentals=0),
    )


def shape(dims, dtype):
    return jax.ShapeDtypeStruct(dims, dtype)


def dot(a, b):
    return lax.dot_general(a, b, (((1,), (0,)), ((), ())), preferred_element_type=F32)


def dot_nt(a, b):
    return lax.dot_general(a, b, (((1,), (1,)), ((), ())), preferred_element_type=F32)


def dot_tn(a, b):
    return lax.dot_general(a, b, (((0,), (0,)), ((), ())), preferred_element_type=F32)


def grad_half(acts, grads, half, extra=None):
    tokens, width = acts.shape
    wide = width // 2
    cols = grads.shape[1]
    tile = 512 if cols % 512 == 0 else 256
    given = [extra] if extra is not None else []

    def kernel(half_ref, a_ref, g_ref, *rest):
        total = dot_tn(a_ref[...], g_ref[...])
        if given:
            total = total + rest[0][...]
        rest[-1][...] = total

    out_block = pl.BlockSpec((wide, tile), lambda j, s: (0, j))
    return call(
        kernel,
        (cols // tile,),
        [
            pl.BlockSpec((tokens, wide), lambda j, s: (0, s[0])),
            pl.BlockSpec((tokens, tile), lambda j, s: (0, j)),
        ]
        + [out_block] * len(given),
        out_block,
        shape((wide, cols), F32),
        prefetch=1,
        flops=2 * tokens * wide * cols,
        bytes_accessed=2 * tokens * (wide + cols) + 4 * wide * cols * (1 + len(given)),
    )(half, acts, grads, *given)


def gather_ids(ids):
    count = lax.axis_size("seq")
    bits = count.bit_length() - 1
    position = lax.axis_index("seq")
    held = ids[None]
    for step in range(bits):
        flip = 1 << step
        other = lax.ppermute(held, "seq", [(i, i ^ flip) for i in range(count)])
        low = (position & flip) == 0
        held = jnp.concatenate([jnp.where(low, held, other), jnp.where(low, other, held)], axis=0)
    return held


def weighted_sums(weights, arrays):
    outs, count, row_count = weights.shape

    def kernel(w_ref, *refs):
        for k in range(outs):
            for r in range(row_count):
                total = None
                for j in range(count):
                    flag = w_ref[(k * count + j) * row_count + r]
                    one = jnp.where(flag > 0.0, refs[j][r], 0.0)
                    total = one if total is None else total + one
                refs[count + k][r] = total

    whole = pl.BlockSpec(memory_space=pltpu.VMEM)
    return pl.pallas_call(
        kernel,
        in_specs=[pl.BlockSpec(memory_space=pltpu.SMEM)] + [whole] * count,
        out_specs=[whole] * outs,
        out_shape=[shape(arrays[0].shape, F32)] * outs,
    )(weights.reshape(-1), *arrays)


def split_shares(state, at, plane):
    row_count, depth, lanes = state.shape
    size = depth // plane

    def kernel(at_ref, s_ref, *outs):
        for k in range(plane):
            begin = pl.multiple_of((at_ref[0] ^ k) * size, size)
            outs[k][...] = s_ref[:, pl.ds(begin, size), :]

    whole = pl.BlockSpec(memory_space=pltpu.VMEM)
    return pl.pallas_call(
        kernel,
        in_specs=[pl.BlockSpec(memory_space=pltpu.SMEM), whole],
        out_specs=[whole] * plane,
        out_shape=[shape((row_count, size, lanes), F32)] * plane,
    )(at, state)


def join_shares(shares, at):
    plane = len(shares)
    row_count, size, lanes = shares[0].shape

    def kernel(at_ref, *refs):
        for k in range(plane):
            begin = pl.multiple_of((at_ref[0] ^ k) * size, size)
            refs[plane][:, pl.ds(begin, size), :] = refs[k][...]

    whole = pl.BlockSpec(memory_space=pltpu.VMEM)
    return pl.pallas_call(
        kernel,
        in_specs=[pl.BlockSpec(memory_space=pltpu.SMEM)] + [whole] * plane,
        out_specs=whole,
        out_shape=shape((row_count, size * plane, lanes), F32),
    )(at, *shares)


def prefix_plan(ids, reverse):
    count = lax.axis_size("seq")
    position = lax.axis_index("seq")
    z_bits, y_bits, x_bits = chip_grid(count)
    planes = 1 << z_bits
    plane = 1 << (y_bits + x_bits)
    z_at, at = position // plane, position % plane
    end = 0 if reverse else plane - 1

    def id_of(index):
        return lax.dynamic_index_in_dim(ids, jnp.clip(index, 0, count - 1), 0, False)

    last = id_of(z_at * plane + end)
    in_plane = [id_of(z_at * plane + (at ^ k)) for k in range(plane)]
    to_total = jnp.stack([one == last for one in in_plane])[None]
    rows = []
    for k in range(plane):
        target_at = at ^ k
        target = z_at * plane + target_at
        near_id = id_of(target + 1 if reverse else target - 1)
        row = []
        for j in range(plane):
            source_at = at ^ j
            before = source_at > target_at if reverse else source_at < target_at
            row.append(before & (in_plane[j] == near_id))
        for step in range(1, planes):
            source = z_at + step if reverse else z_at - step
            there = (source >= 0) & (source < planes)
            row.append(there & (id_of(source * plane + end) == near_id))
        rows.append(jnp.stack(row))
    near = position + 1 if reverse else position - 1
    near_id = jnp.where((near < count) & (near >= 0), id_of(near), -1.0)
    return to_total.astype(F32), jnp.stack(rows).astype(F32), near_id


def prefix(state, to_total, to_results, reverse):
    count = lax.axis_size("seq")
    z_bits, y_bits, x_bits = chip_grid(count)
    planes = 1 << z_bits
    plane = 1 << (y_bits + x_bits)
    at = (lax.axis_index("seq") % plane).astype(jnp.int32).reshape(1)

    def swap(shares):
        return [shares[0]] + [
            lax.ppermute(
                shares[k], "seq", [(i, (i // plane) * plane + ((i % plane) ^ k)) for i in range(count)]
            )
            for k in range(1, plane)
        ]

    swapped = swap(split_shares(state, at, plane))
    (total,) = weighted_sums(to_total, swapped)
    passed = []
    for step in range(1, planes):
        shift = -step * plane if reverse else step * plane
        moves = [(i, i + shift) for i in range(count) if 0 <= i + shift < count]
        passed.append(lax.ppermute(total, "seq", moves))
    return join_shares(swap(weighted_sums(to_results, swapped + passed)), at)


def softplus(v):
    return jnp.maximum(v, 0.0) + jnp.log1p(jnp.exp(-jnp.abs(v)))


def sigmoid(v):
    return 1.0 / (1.0 + jnp.exp(-v))


def sigmoid_of_softplus(s):
    return jnp.where(s < 0.01, s * (1.0 - s * (0.5 - s * (1.0 / 6.0))), 1.0 - jnp.exp(-s))


def mean_square(v):
    return jnp.mean(v * v, axis=-1, keepdims=True)


def head_ones():
    a = lax.broadcasted_iota(jnp.int32, (GROUP, GROUP), 0) >> 6
    b = lax.broadcasted_iota(jnp.int32, (GROUP, GROUP), 1) >> 6
    return jnp.where(a == b, 1.0 / HEAD_DIM, 0.0).astype(BF16)


def head_mean(v, ones):
    high = v.astype(BF16)
    low = (v - high.astype(F32)).astype(BF16)
    return dot(high, ones) + dot(low, ones)


def one_head(block, h):
    lanes = lax.broadcasted_iota(jnp.int32, (1, GROUP), 1) >> 6
    return jnp.where(lanes == h, block, jnp.zeros_like(block))


def pack_state(full):
    left = lax.broadcasted_iota(jnp.int32, (HEAD_DIM, 128), 1) < HEAD_DIM
    pairs = []
    for p in range(2):
        block = full[128 * p : 128 * p + 128, 128 * p : 128 * p + 128]
        pairs.append(jnp.where(left, block[:HEAD_DIM], block[HEAD_DIM:]))
    return jnp.concatenate(pairs, axis=0)


def unpack_state(packed):
    left = lax.broadcasted_iota(jnp.int32, (HEAD_DIM, 128), 1) < HEAD_DIM
    none = jnp.zeros((128, 128), F32)
    rows = []
    for p in range(2):
        block = packed[HEAD_DIM * p : HEAD_DIM * p + HEAD_DIM]
        square = jnp.concatenate([jnp.where(left, block, 0.0), jnp.where(left, 0.0, block)], axis=0)
        rows.append(jnp.concatenate([square, none] if p == 0 else [none, square], axis=1))
    return jnp.concatenate(rows, axis=0).astype(BF16)


def full_spec(dims):
    return pl.BlockSpec(dims, lambda *_: (0,) * len(dims))


def column_spec(tokens, tile):
    return pl.BlockSpec((tokens, tile), lambda j, *_: (0, j))


def row_spec(tile, width):
    return pl.BlockSpec((tile, width), lambda i, *_: (i, 0))


SMEM = pl.BlockSpec(memory_space=pltpu.SMEM)


def project_keys(inputs, ids_col, last_ids, w_key, w_value, row_count):
    tokens, width = inputs.shape
    block = tokens // row_count

    def kernel(last_ref, x_ref, id_ref, wk_ref, wv_ref, xn_ref, k_ref, v_ref, s_ref):
        @pl.when(pl.program_id(0) == 0)
        def _():
            for i in range(tokens // TILE):
                x = x_ref[pl.ds(i * TILE, TILE), :].astype(F32)
                xn_ref[pl.ds(i * TILE, TILE), :] = (x * lax.rsqrt(mean_square(x) + EPSILON)).astype(BF16)

        xn = xn_ref[...]
        keys = softplus(dot(xn, wk_ref[...])).astype(BF16)
        values = dot(xn, wv_ref[...]).astype(BF16)
        k_ref[...] = keys
        v_ref[...] = values
        for r in range(row_count):
            at = slice(r * block, (r + 1) * block)
            kept = jnp.where(id_ref[at] == last_ref[r], keys[at], jnp.zeros((), BF16))
            s_ref[r] = pack_state(dot_tn(kept, values[at]))

    return call(
        kernel,
        (width // GROUP,),
        [SMEM, full_spec((tokens, width)), full_spec((tokens, 1)), column_spec(width, GROUP), column_spec(width, GROUP)],
        [
            full_spec((tokens, width)),
            column_spec(tokens, GROUP),
            column_spec(tokens, GROUP),
            pl.BlockSpec((row_count, GROUP // 2, 128), lambda j: (0, j, 0)),
        ],
        [shape((tokens, width), BF16)] * 3 + [shape((row_count, width // 2, 128), F32)],
        flops=4 * tokens * width * width,
        bytes_accessed=12 * tokens * width,
    )(last_ids, inputs, ids_col, w_key, w_value)


def block_mask(id_col, id_row, first, transposed):
    dims = (id_col.shape[0], id_row.shape[1])
    a = lax.broadcasted_iota(jnp.int32, dims, 0) + first
    b = lax.broadcasted_iota(jnp.int32, dims, 1)
    causal = b >= a if transposed else a >= b
    return jnp.where(causal & (id_col == id_row), 1.0, 0.0).astype(BF16)


def attend(normed, keys, values, ids_col, ids_row, w_query, w_outgate):
    tokens, width = normed.shape
    row_count, _, block = ids_row.shape

    def kernel(xn_ref, k_ref, v_ref, ic_ref, ir_ref, wq_ref, wg_ref, q_ref, g_ref, o_ref, mask_ref):
        @pl.when(pl.program_id(0) == 0)
        def _():
            for r in range(row_count):
                for i in range(block // TILE):
                    at = pl.ds(r * block + i * TILE, TILE)
                    mask_ref[at, :] = block_mask(ic_ref[at, :], ir_ref[r], i * TILE, False)

        xn = xn_ref[...]
        q_ref[...] = softplus(dot(xn, wq_ref[...])).astype(BF16)
        g_ref[...] = sigmoid(dot(xn, wg_ref[...])).astype(BF16)
        for r in range(row_count):
            base = r * block
            for i in range(block // TILE):
                rows = pl.ds(base + i * TILE, TILE)
                seen = (i + 1) * TILE
                q = q_ref[rows, :]
                mask = mask_ref[rows, pl.ds(0, seen)]
                total = None
                for h in range(4):
                    k = one_head(k_ref[pl.ds(base, seen), :], h)
                    v = one_head(v_ref[pl.ds(base, seen), :], h)
                    scores = dot_nt(q, k).astype(BF16) * mask
                    one = dot(scores, v)
                    total = one if total is None else total + one
                o_ref[rows, :] = total

    return call(
        kernel,
        (width // GROUP,),
        [
            full_spec((tokens, width)),
            column_spec(tokens, GROUP),
            column_spec(tokens, GROUP),
            full_spec((tokens, 1)),
            full_spec((row_count, 1, block)),
            column_spec(width, GROUP),
            column_spec(width, GROUP),
        ],
        [column_spec(tokens, GROUP)] * 3,
        [shape((tokens, width), BF16)] * 2 + [shape((tokens, width), F32)],
        scratch=[pltpu.VMEM((tokens, block), BF16)],
        flops=4 * tokens * width * width + 16 * tokens * block * width // 2,
        bytes_accessed=18 * tokens * width,
    )(normed, keys, values, ids_col, ids_row, w_query, w_outgate)


def combine(queries, inside, gates, inputs, carried, near_ids, ids_col, head_gain, w_output):
    tokens, width = queries.shape
    row_count = carried.shape[0]
    block = tokens // row_count
    per_row = block // TILE

    def kernel(near_ref, q_ref, in_ref, g_ref, x_ref, c_ref, id_ref, gain_ref, wo_ref, at_ref, go_ref, h_ref, nm_ref):
        near = near_ref[pl.program_id(0) // per_row]
        matched = id_ref[...] == near
        ones = head_ones()
        for j in range(width // GROUP):
            cols = pl.ds(j * GROUP, GROUP)
            state = unpack_state(c_ref[0, pl.ds(j * GROUP // 2, GROUP // 2), :])
            across = dot(q_ref[:, cols], state)
            attended = in_ref[:, cols] + jnp.where(matched, across, 0.0)
            at_ref[:, cols] = attended.astype(BF16)
            unit = attended * lax.rsqrt(head_mean(attended * attended, ones) + EPSILON)
            go_ref[:, cols] = (unit * gain_ref[:, cols] * g_ref[:, cols].astype(F32)).astype(BF16)
        hidden = x_ref[...].astype(F32) + dot(go_ref[...], wo_ref[...])
        h_ref[...] = hidden
        nm_ref[...] = (hidden * lax.rsqrt(mean_square(hidden) + EPSILON)).astype(BF16)

    tile = row_spec(TILE, width)
    return call(
        kernel,
        (tokens // TILE,),
        [
            SMEM,
            tile,
            tile,
            tile,
            tile,
            pl.BlockSpec((1, width // 2, 128), lambda i: (i // per_row, 0, 0)),
            row_spec(TILE, 1),
            full_spec((1, width)),
            full_spec((width, width)),
        ],
        [tile] * 4,
        [shape((tokens, width), BF16)] * 2 + [shape((tokens, width), F32), shape((tokens, width), BF16)],
        flops=2 * tokens * width * width,
        bytes_accessed=20 * tokens * width + 2 * width * width,
    )(near_ids, queries, inside, gates, inputs, carried, ids_col, head_gain, w_output)


def gate_up(normed, w_gate, w_up):
    tokens, width = normed.shape
    wide = w_gate.shape[1]

    def kernel(n_ref, wg_ref, wu_ref, g_ref, u_ref, p_ref):
        n = n_ref[...]
        gate = dot(n, wg_ref[...])
        up = dot(n, wu_ref[...])
        g_ref[...] = gate.astype(BF16)
        u_ref[...] = up.astype(BF16)
        p_ref[...] = (gate * up).astype(BF16)

    return call(
        kernel,
        (wide // TILE,),
        [full_spec((tokens, width)), column_spec(width, TILE), column_spec(width, TILE)],
        [column_spec(tokens, TILE)] * 3,
        [shape((tokens, wide), BF16)] * 3,
        flops=4 * tokens * width * wide,
        bytes_accessed=4 * width * wide + 6 * tokens * wide,
    )(normed, w_gate, w_up)


def back_gate_up(cotangent, w_down, gate, up, begin, end):
    tokens, width = cotangent.shape
    count = end - begin

    def kernel(c_ref, wd_ref, g_ref, u_ref, o_ref):
        back = dot_nt(c_ref[...], wd_ref[...])
        o_ref[:, pl.ds(0, TILE)] = (back * u_ref[...].astype(F32)).astype(BF16)
        o_ref[:, pl.ds(TILE, TILE)] = (back * g_ref[...].astype(F32)).astype(BF16)

    part = pl.BlockSpec((tokens, TILE), lambda j: (0, j + begin))
    return call(
        kernel,
        (count,),
        [full_spec((tokens, width)), pl.BlockSpec((TILE, width), lambda j: (j + begin, 0)), part, part],
        column_spec(tokens, 2 * TILE),
        shape((tokens, 2 * TILE * count), BF16),
        flops=2 * tokens * width * TILE * count,
        bytes_accessed=(8 * tokens + 2 * width) * TILE * count,
    )(cotangent, w_down, gate, up)


def block_output(hidden, product, w_down):
    tokens, width = hidden.shape
    wide = product.shape[1]

    def kernel(h_ref, p_ref, w_ref, o_ref):
        o_ref[...] = (h_ref[...] + dot(p_ref[...], w_ref[...])).astype(BF16)

    return call(
        kernel,
        (tokens // TILE,),
        [row_spec(TILE, width), row_spec(TILE, wide), full_spec((wide, width))],
        row_spec(TILE, width),
        shape((tokens, width), BF16),
        flops=2 * tokens * width * wide,
        bytes_accessed=6 * tokens * width + 2 * wide * (tokens + width),
    )(hidden, product, w_down)


def norm_back(unit, scale, grad):
    return scale * (grad - unit * jnp.mean(grad * unit, axis=-1, keepdims=True))


def back_mid_heads(
    backs, w_gate, w_up, cotangent, hidden, w_output, attended, gates, head_gain, queries, first_ids, ids_col, row_count
):
    tokens, width = cotangent.shape
    block = tokens // row_count
    per_row = block // TILE
    counts = [b.shape[1] // (2 * TILE) for b in backs]
    steps = sum(counts)
    begins = [sum(counts[:i]) for i in range(len(counts))]
    number = len(backs)

    def kernel(first_ref, *refs):
        b_refs = refs[:number]
        (wg_ref, wu_ref, c_ref, h_ref, wo_ref, at_ref, g_ref, gain_ref, q_ref, id_ref) = refs[number : number + 10]
        (bb_ref, bo_ref, ba_ref, gg_ref, s_ref, acc_ref) = refs[number + 10 :]
        step = pl.program_id(0)

        @pl.when(step == 0)
        def _():
            acc_ref[...] = jnp.zeros_like(acc_ref)

        for b_ref, begin, count in zip(b_refs, begins, counts):

            @pl.when((step >= begin) & (step < begin + count))
            def _(b_ref=b_ref):
                w = jnp.concatenate([wg_ref[...], wu_ref[...]], axis=1)
                acc_ref[...] += dot_nt(b_ref[...], w)

        @pl.when(step == steps - 1)
        def _():
            ones = head_ones()
            gains = [jnp.zeros((1, GROUP), F32)] * (width // GROUP)
            for r in range(row_count):
                sums = [None] * (width // GROUP)
                for i in range(per_row):
                    rows = pl.ds(r * block + i * TILE, TILE)
                    h = h_ref[rows, :]
                    scale = lax.rsqrt(mean_square(h) + EPSILON)
                    back = c_ref[rows, :].astype(F32) + norm_back(h * scale, scale, acc_ref[rows, :])
                    bb_ref[rows, :] = back.astype(BF16)
                    acc_ref[rows, :] = dot_nt(bb_ref[rows, :], wo_ref[...])
                    in_first = id_ref[rows, :] == first_ref[r]
                    for j in range(width // GROUP):
                        cols = pl.ds(j * GROUP, GROUP)
                        attended = at_ref[rows, cols].astype(F32)
                        scale_h = lax.rsqrt(head_mean(attended * attended, ones) + EPSILON)
                        unit = attended * scale_h
                        gate = g_ref[rows, cols].astype(F32)
                        gain = gain_ref[:, cols]
                        gated = acc_ref[rows, cols] * gate
                        along = unit * gated
                        gains[j] = gains[j] + jnp.sum(along, axis=0, keepdims=True)
                        bo_ref[rows, cols] = (along * gain * (1.0 - gate)).astype(BF16)
                        back_unit = gated * gain
                        mean = head_mean(back_unit * unit, ones)
                        ba = (scale_h * (back_unit - unit * mean)).astype(BF16)
                        ba_ref[rows, cols] = ba
                        q = jnp.where(in_first, q_ref[rows, cols], jnp.zeros((), BF16))
                        one = dot_tn(q, ba)
                        sums[j] = one if sums[j] is None else sums[j] + one
                for j in range(width // GROUP):
                    s_ref[r, pl.ds(j * GROUP // 2, GROUP // 2), :] = pack_state(sums[j])
            for j in range(width // GROUP):
                gg_ref[:, pl.ds(j * GROUP, GROUP)] = gains[j]

    def chunk_spec(begin, count):
        return pl.BlockSpec((tokens, 2 * TILE), lambda j: (0, jnp.clip(j - begin, 0, count - 1)))

    whole = full_spec((tokens, width))
    weights = column_spec(width, TILE)
    return call(
        kernel,
        (steps,),
        [SMEM]
        + [chunk_spec(b, c) for b, c in zip(begins, counts)]
        + [weights, weights, whole, whole, full_spec((width, width)), whole, whole, full_spec((1, width)), whole]
        + [full_spec((tokens, 1))],
        [whole] * 3 + [full_spec((1, width)), full_spec((row_count, width // 2, 128))],
        [shape((tokens, width), BF16)] * 3 + [shape((1, width), F32), shape((row_count, width // 2, 128), F32)],
        scratch=[pltpu.VMEM((tokens, width), F32)],
        flops=4 * tokens * width * TILE * steps + 2 * tokens * width * width,
        bytes_accessed=4 * (tokens + width) * TILE * steps + 24 * tokens * width,
    )(first_ids, *backs, w_gate, w_up, cotangent, hidden, w_output, attended, gates, head_gain, queries, ids_col)


def attend_back(queries, keys, values, back_attended, carried, near_ids, ids_col, ids_row):
    tokens, width = queries.shape
    row_count, _, block = ids_row.shape

    def kernel(near_ref, q_ref, k_ref, v_ref, a_ref, c_ref, ic_ref, ir_ref, bq_ref, bk_ref, bv_ref, mask_ref, flip_ref):
        @pl.when(pl.program_id(0) == 0)
        def _():
            for r in range(row_count):
                for i in range(block // TILE):
                    at = pl.ds(r * block + i * TILE, TILE)
                    mask_ref[at, :] = block_mask(ic_ref[at, :], ir_ref[r], i * TILE, False)
                    flip_ref[at, :] = block_mask(ic_ref[at, :], ir_ref[r], i * TILE, True)

        for r in range(row_count):
            base = r * block
            state = unpack_state(c_ref[r])
            for i in range(block // TILE):
                rows = pl.ds(base + i * TILE, TILE)
                seen = (i + 1) * TILE
                earlier = pl.ds(base, seen)
                later = pl.ds(base + i * TILE, block - i * TILE)
                a = a_ref[rows, :]
                q = q_ref[rows, :]
                k = k_ref[rows, :]
                v = v_ref[rows, :]
                matched = ic_ref[rows, :] == near_ref[r]
                back_q = jnp.where(matched, dot_nt(a, state), 0.0)
                back_k = None
                back_v = None
                mask = mask_ref[rows, pl.ds(0, seen)]
                flip = flip_ref[rows, pl.ds(i * TILE, block - i * TILE)]
                for h in range(4):
                    grads = dot_nt(a, one_head(v_ref[earlier, :], h)).astype(BF16) * mask
                    back_q = back_q + dot(grads, one_head(k_ref[earlier, :], h))
                    q_h = one_head(q_ref[later, :], h)
                    a_h = one_head(a_ref[later, :], h)
                    scores_t = dot_nt(k, q_h).astype(BF16) * flip
                    grads_t = dot_nt(v, a_h).astype(BF16) * flip
                    one = dot(grads_t, q_h)
                    back_k = one if back_k is None else back_k + one
                    one = dot(scores_t, a_h)
                    back_v = one if back_v is None else back_v + one
                bq_ref[rows, :] = (back_q * sigmoid_of_softplus(q.astype(F32))).astype(BF16)
                bk_ref[rows, :] = back_k
                bv_ref[rows, :] = back_v

    tile = column_spec(tokens, GROUP)
    return call(
        kernel,
        (width // GROUP,),
        [SMEM, tile, tile, tile, tile, pl.BlockSpec((row_count, GROUP // 2, 128), lambda j: (0, j, 0))]
        + [full_spec((tokens, 1)), full_spec((row_count, 1, block))],
        [tile] * 3,
        [shape((tokens, width), BF16)] + [shape((tokens, width), F32)] * 2,
        scratch=[pltpu.VMEM((tokens, block), BF16)] * 2,
        flops=48 * tokens * block * width // 2,
        bytes_accessed=18 * tokens * width,
    )(near_ids, queries, keys, values, back_attended, carried, ids_col, ids_row)


def finish_keys(back_k, back_v, keys, values, state_grad, near_ids, ids_col):
    tokens, width = keys.shape
    row_count = state_grad.shape[0]
    block = tokens // row_count

    def kernel(near_ref, bk_ref, bv_ref, k_ref, v_ref, s_ref, id_ref, ok_ref, ov_ref):
        for r in range(row_count):
            rows = pl.ds(r * block, block)
            state = unpack_state(s_ref[r])
            uses = id_ref[rows, :] == near_ref[r]
            k = k_ref[rows, :]
            back_k = bk_ref[rows, :] + jnp.where(uses, dot_nt(v_ref[rows, :], state), 0.0)
            ok_ref[rows, :] = (back_k * sigmoid_of_softplus(k.astype(F32))).astype(BF16)
            ov_ref[rows, :] = (bv_ref[rows, :] + jnp.where(uses, dot(k, state), 0.0)).astype(BF16)

    tile = column_spec(tokens, GROUP)
    return call(
        kernel,
        (width // GROUP,),
        [SMEM, tile, tile, tile, tile, pl.BlockSpec((row_count, GROUP // 2, 128), lambda j: (0, j, 0))]
        + [full_spec((tokens, 1))],
        [tile] * 2,
        [shape((tokens, width), BF16)] * 2,
        flops=4 * tokens * GROUP * width,
        bytes_accessed=16 * tokens * width,
    )(near_ids, back_k, back_v, keys, values, state_grad, ids_col)


def input_gradient(grads, weights, inputs, back_branch):
    tokens, width = inputs.shape

    def kernel(a_ref, b_ref, c_ref, d_ref, wa_ref, wb_ref, wc_ref, wd_ref, x_ref, bb_ref, o_ref):
        back = dot_nt(a_ref[...], wa_ref[...]) + dot_nt(b_ref[...], wb_ref[...])
        back = back + dot_nt(c_ref[...], wc_ref[...]) + dot_nt(d_ref[...], wd_ref[...])
        x = x_ref[...].astype(F32)
        scale = lax.rsqrt(mean_square(x) + EPSILON)
        o_ref[...] = (bb_ref[...].astype(F32) + norm_back(x * scale, scale, back)).astype(BF16)

    tile = row_spec(TILE, width)
    return call(
        kernel,
        (tokens // TILE,),
        [tile] * 4 + [full_spec((width, width))] * 4 + [tile] * 2,
        tile,
        shape((tokens, width), BF16),
        flops=8 * tokens * width * width,
        bytes_accessed=14 * tokens * width + 8 * width * width,
    )(*grads, *weights, inputs, back_branch)


def local(
    inputs,
    doc_ids,
    w_query,
    w_key,
    w_value,
    w_outgate,
    w_output,
    w_gate,
    w_up,
    w_down,
    head_gain,
    cotangent,
):
    row_count, block_len, width = inputs.shape
    tokens = row_count * block_len
    x_first, y_first, z_first = orders(lax.axis_size("seq"))
    core = lax.axis_index("batch").astype(jnp.int32).reshape(1)
    x_flat = inputs.reshape(tokens, width)
    cot_flat = cotangent.reshape(tokens, width)
    gain = head_gain.reshape(1, width)
    ids = doc_ids.astype(F32)
    ids_col = ids.reshape(tokens, 1)
    ids_row = ids.reshape(row_count, 1, block_len)
    first_ids, last_ids = ids[:, 0], ids[:, -1]
    edge_ids = gather_ids(jnp.concatenate([first_ids, last_ids]))
    before_total, before_results, before_ids = prefix_plan(edge_ids[:, row_count:], False)
    after_total, after_results, after_ids = prefix_plan(edge_ids[:, :row_count], True)

    def half_sum(acts, grads):
        received = to_core(grad_half(acts, grads, 1 - core))
        return grad_half(acts, grads, core, received)

    normed, keys, values, state = project_keys(x_flat, ids_col, last_ids, w_key, w_value, row_count)
    carried = prefix(state, before_total, before_results, False)
    queries, gates, inside = attend(normed, keys, values, ids_col, ids_row, w_query, w_outgate)
    attended, gated, hidden, normed_mid = combine(
        queries, inside, gates, x_flat, carried, before_ids, ids_col, gain, w_output
    )
    gate, up, product = gate_up(normed_mid, w_gate, w_up)

    half_down = half_sum(product, cot_flat)
    grad_down = jnp.concatenate(
        [
            scatter_seq([half_down], x_first, (0, width // 2)),
            scatter_seq([half_down], y_first, (width // 2, width)),
        ],
        axis=1,
    )

    tiles = w_gate.shape[1] // TILE
    cuts = [0, tiles // 2, tiles]
    backs = [back_gate_up(cot_flat, w_down, gate, up, a, b) for a, b in zip(cuts[:-1], cuts[1:])]
    wide_parts = []
    for back, order in zip(backs, (z_first, None)):
        half = half_sum(normed_mid, back)
        n = half.shape[1]
        if order is not None:
            done = scatter_seq([half], order)
        else:
            middle = n // 2
            done = jnp.concatenate(
                [scatter_seq([half], x_first, (0, middle)), scatter_seq([half], y_first, (middle, n))], axis=1
            )
        wide_parts.append(done.reshape(done.shape[0], n // (2 * TILE), 2, TILE))
    wide = jnp.concatenate(wide_parts, axis=1)
    grad_gate = wide[:, :, 0].reshape(wide.shape[0], tiles * TILE)
    grad_up = wide[:, :, 1].reshape(wide.shape[0], tiles * TILE)

    back_branch, back_outgate, back_attended, gain_terms, state_out = back_mid_heads(
        backs, w_gate, w_up, cot_flat, hidden, w_output, attended, gates, gain, queries, first_ids, ids_col, row_count
    )
    state_grad = prefix(state_out, after_total, after_results, True)
    grad_output = scatter_seq([half_sum(gated, back_branch)], x_first)
    grad_outgate = scatter_seq([half_sum(normed, back_outgate)], y_first)
    back_query, part_key, part_value = attend_back(
        queries, keys, values, back_attended, carried, before_ids, ids_col, ids_row
    )
    grad_query = scatter_seq([half_sum(normed, back_query)], x_first)
    back_key, back_value = finish_keys(part_key, part_value, keys, values, state_grad, after_ids, ids_col)
    grad_key = scatter_seq([half_sum(normed, back_key)], y_first)
    grad_value = scatter_seq([half_sum(normed, back_value)], x_first)

    gain_halves = gain_terms.reshape(2, width // 2)
    gain_sent = to_core(lax.dynamic_index_in_dim(gain_halves, 1 - core[0], 0, False))
    gain_kept = lax.dynamic_index_in_dim(gain_halves, core[0], 0, False) + gain_sent
    grad_gain = scatter_seq([gain_kept], x_first)

    block_out = block_output(hidden, product, w_down).reshape(inputs.shape)
    input_grad = input_gradient(
        (back_query, back_key, back_value, back_outgate), (w_query, w_key, w_value, w_outgate), x_flat, back_branch
    ).reshape(inputs.shape)
    return (
        block_out,
        input_grad,
        grad_query,
        grad_key,
        grad_value,
        grad_outgate,
        grad_output,
        grad_gate,
        grad_up,
        grad_down,
        grad_gain,
    )


def solution(mesh):
    rows = P("batch", "seq", None)
    scattered = P(("batch", "seq"), None)
    return jax.shard_map(
        local,
        mesh=mesh,
        in_specs=(rows, P("batch", "seq")) + (P(),) * 9 + (rows,),
        out_specs=(rows, rows) + (scattered,) * 8 + (P(("batch", "seq")),),
        check_vma=False,
    )
```

```python
import functools

import jax
import jax.numpy as jnp
from jax import lax
from jax.experimental import pallas as pl
from jax.experimental.pallas import tpu as pltpu
from jax.sharding import PartitionSpec as P

HEADS = 16
HEAD_DIM = 64
GROUP = 4 * HEAD_DIM
TILE = 256
EPSILON = 1e-06
F32 = jnp.float32
BF16 = jnp.bfloat16
VMEM_BYTES = 56 << 20
FLOPS_US = 1e11
STEPS = 2


def chip_grid(count):
    bits = count.bit_length() - 1
    z_bits = min(bits, 2)
    y_bits = (bits - z_bits + 1) // 2
    return z_bits, y_bits, bits - z_bits - y_bits


def orders(count):
    z_bits, y_bits, x_bits = chip_grid(count)
    z_axes = list(range(z_bits))[::-1]
    y_axes = list(range(z_bits, z_bits + y_bits))[::-1]
    x_axes = list(range(z_bits + y_bits, z_bits + y_bits + x_bits))[::-1]
    return x_axes + y_axes, y_axes + x_axes, z_axes


class Scatter:
    def __init__(self, turns, halves, order):
        self.turns = turns
        self.count = lax.axis_size("seq")
        self.bits = self.count.bit_length() - 1
        self.position = lax.axis_index("seq").astype(jnp.int32).reshape(1)
        self.rows = halves[0][0].shape[0] // self.count
        axes = tuple(range(self.bits))
        self.parts = [
            ([h.reshape((self.count, self.rows, h.shape[1])) for h in half], axes) for half in halves
        ]
        self.order = list(order)
        self.done = ()

    def total(self, flipped, widths=None):
        fixed = self.done if flipped is None else self.done + (flipped,)
        left = tuple(a for a in range(self.bits) if a not in fixed)
        bits, done = self.bits, self.done

        def block(axes, j, position):
            at = 0
            for a in axes:
                if a in left:
                    bit = (j >> (len(left) - 1 - left.index(a))) & 1
                else:
                    bit = (position[0] >> (bits - 1 - a)) & 1
                    if a == flipped:
                        bit = 1 - bit
                at = at * 2 + bit
            return at

        count = 1 << len(left)
        deep = max(1, count // STEPS)
        arrays, specs, places = [], [], []
        for held, axes in self.parts:
            begin = 0
            for array in held:
                wide = array.shape[2]
                for d in range(deep):
                    arrays.append(array)
                    specs.append(
                        pl.BlockSpec(
                            (1, self.rows, wide),
                            lambda j, position, axes=axes, d=d: (block(axes, j * deep + d, position), 0, 0),
                        )
                    )
                    places.append((d, begin, begin + wide))
                begin += wide
        final = widths is not None
        widths = widths or [begin]

        def kernel(position_ref, *refs):
            ins, outs = refs[: len(arrays)], refs[len(arrays) :]
            edge = 0
            for out, wide in zip(outs, widths):
                covers = sorted({p[1:] for p in places if p[1] < edge + wide and p[2] > edge})
                smallest = [p for p in covers if not any(q != p and p[0] <= q[0] and q[1] <= p[1] for q in covers)]
                for d in range(deep):
                    for low, high in smallest:
                        low, high = max(low, edge), min(high, edge + wide)
                        one = None
                        for ref, (at, begin, stop) in zip(ins, places):
                            if at == d and begin <= low and high <= stop:
                                term = ref[0, :, pl.ds(low - begin, high - low)]
                                one = term if one is None else one + term
                        if final:
                            out[:, pl.ds(low - edge, high - low)] = one
                        else:
                            out[d, :, pl.ds(low - edge, high - low)] = one
                edge += wide

        if final:
            out_specs = [pl.BlockSpec((self.rows, w), lambda j, position: (0, 0)) for w in widths]
            out_shape = [shape((self.rows, w), F32) for w in widths]
        else:
            out_specs = [pl.BlockSpec((deep, self.rows, w), lambda j, position: (j, 0, 0)) for w in widths]
            out_shape = [shape((count, self.rows, w), F32) for w in widths]
        return self.turns.call(kernel, (count // deep,), specs, out_specs, out_shape, prefetch=1, us=2)(
            self.position, *arrays
        )

    def finish_planes(self):
        while self.order:
            self.step()
        (terms,) = self.total(None)
        return scatter_between_planes(terms.reshape(-1, terms.shape[2]))

    def step(self):
        axis = self.order.pop(0)
        (outgoing,) = self.total(axis)
        flip = 1 << (self.bits - 1 - axis)
        incoming = lax.ppermute(outgoing, "seq", [(i, i ^ flip) for i in range(self.count)])
        self.done = self.done + (axis,)
        left = tuple(a for a in range(self.bits) if a not in self.done)
        self.parts.append(([incoming], left))

    def finish(self, *widths):
        while self.order:
            self.step()
        return self.total(None, list(widths))


def to_core(arrays):
    return [lax.ppermute(array, "batch", [(0, 1), (1, 0)]) for array in arrays]


class Turns:
    def __init__(self):
        self.last = ()

    def call(self, kernel, grid, in_specs, out_specs, out_shape, scratch=(), prefetch=0, us=10):
        given = len(in_specs) + prefetch
        waits = len(self.last)

        def body(*refs):
            kernel(*refs[:given], *refs[given + waits :])

        spec = pltpu.PrefetchScalarGridSpec(
            num_scalar_prefetch=prefetch,
            grid=grid,
            in_specs=list(in_specs) + [pl.BlockSpec(memory_space=pl.ANY)] * waits,
            out_specs=out_specs,
            scratch_shapes=scratch,
        )

        def run(*args):
            out = pl.pallas_call(
                body,
                grid_spec=spec,
                out_shape=out_shape,
                compiler_params=pltpu.CompilerParams(vmem_limit_bytes=VMEM_BYTES),
                cost_estimate=pl.CostEstimate(flops=int(us * FLOPS_US), bytes_accessed=0, transcendentals=0),
            )(*args, *self.last)
            self.last = (out[0] if isinstance(out, (list, tuple)) else out,)
            return out

        return run


def shape(dims, dtype):
    return jax.ShapeDtypeStruct(dims, dtype)


def dot(a, b):
    return lax.dot_general(a, b, (((1,), (0,)), ((), ())), preferred_element_type=F32)


def dot_nt(a, b):
    return lax.dot_general(a, b, (((1,), (1,)), ((), ())), preferred_element_type=F32)


def dot_tn(a, b):
    return lax.dot_general(a, b, (((0,), (0,)), ((), ())), preferred_element_type=F32)


def grad_halves(turns, pairs, core, tile, apart=False, us=10):
    tokens, width = pairs[0][0].shape
    wide = width // 2
    per = pairs[0][1].shape[1] // tile
    acts = []
    for one, _ in pairs:
        if not any(one is a for a in acts):
            acts.append(one)
    number, kinds = len(pairs), len(acts)
    which = [[one is a for a in acts].index(True) for one, _ in pairs]
    one_buffer = pl.Buffered(1)
    sent_half = pl.BlockSpec((tokens, wide), lambda j, s: (0, 1 - s[0]), pipeline_mode=one_buffer)
    kept_half = pl.BlockSpec((tokens, wide), lambda j, s: (0, s[0]), pipeline_mode=one_buffer)

    def kernel(core_ref, *refs):
        step = pl.program_id(0)
        outs = refs[2 * kinds + number :]
        for i in range(number):

            @pl.when((step >= i * per) & (step < (i + 1) * per))
            def _(i=i):
                grads = refs[2 * kinds + i][...]
                outs[i if apart else 0][...] = dot_tn(refs[2 * which[i]][...], grads)
                outs[number + i if apart else 1][...] = dot_tn(refs[2 * which[i] + 1][...], grads)

    def part(i):
        return pl.BlockSpec((tokens, tile), lambda j, s: (0, jnp.clip(j - i * per, 0, per - 1)))

    def out_part(i):
        if not apart:
            return pl.BlockSpec((wide, tile), lambda j, s: (0, j))
        return pl.BlockSpec((wide, tile), lambda j, s: (0, jnp.clip(j - i * per, 0, per - 1)))

    arrays = number if apart else 1
    cols = tile * per if apart else tile * per * number
    outs = turns.call(
        kernel,
        (per * number,),
        [sent_half, kept_half] * kinds + [part(i) for i in range(number)],
        [out_part(i) for i in range(arrays)] * 2,
        [shape((wide, cols), F32)] * (2 * arrays),
        prefetch=1,
        us=us,
    )(core, *[a for one in acts for a in (one, one)], *[g for _, g in pairs])
    return list(outs[:arrays]), list(outs[arrays:])


def scatter_between_planes(array):
    count = lax.axis_size("seq")
    planes = 1 << chip_grid(count)[0]
    plane = count // planes
    groups = [[k + plane * z for z in range(planes)] for k in range(plane)]
    return lax.psum_scatter(array, "seq", scatter_dimension=0, axis_index_groups=groups, tiled=True)


def small_call(turns, kernel, out_shape, args):
    def whole(array):
        return pl.BlockSpec(array.shape, lambda _: (0,) * len(array.shape))

    specs = [pl.BlockSpec(memory_space=pltpu.SMEM)] + [whole(a) for a in args[1:]]
    return turns.call(kernel, (1,), specs, [whole(o) for o in out_shape], out_shape, us=2)(*args)


class Prefix:
    def __init__(self, turns, state, edge_ids, reverse):
        self.turns = turns
        self.reverse = reverse
        self.count = lax.axis_size("seq")
        z_bits, y_bits, x_bits = chip_grid(self.count)
        self.planes = 1 << z_bits
        self.plane = plane = 1 << (y_bits + x_bits)
        position = lax.axis_index("seq")
        place = jnp.stack([position // plane, position % plane]).astype(jnp.int32)
        self.place = jnp.concatenate([place, edge_ids])
        row_count, depth, lanes = state.shape
        self.size = size = depth // plane
        self.row_count = row_count
        self.share = shape((row_count, size + 8, lanes), F32)

        def split(at_ref, s_ref, *outs):
            for k in range(plane):
                begin = pl.multiple_of((at_ref[1] ^ k) * size, size)
                outs[k][:, pl.ds(0, size), :] = s_ref[:, pl.ds(begin, size), :]
                for r in range(row_count):
                    outs[k][r, pl.ds(size, 8), :] = jnp.full((8, lanes), at_ref[2 + r].astype(F32))

        shares = small_call(turns, split, [self.share] * plane, (self.place, state))
        self.swapped = self.swap(shares)

    def swap(self, shares):
        plane = self.plane
        return [shares[0]] + [
            lax.ppermute(
                shares[k],
                "seq",
                [(i, (i // plane) * plane + ((i % plane) ^ k)) for i in range(self.count)],
            )
            for k in range(1, plane)
        ]

    def pass_on(self):
        plane, size = self.plane, self.size
        end = 0 if self.reverse else plane - 1

        def total(at_ref, *refs):
            out = refs[plane]
            for r in range(self.row_count):
                last = refs[0][r, pl.ds(size, 8), :]
                for k in range(1, plane):
                    last = jnp.where((at_ref[1] ^ k) == end, refs[k][r, pl.ds(size, 8), :], last)
                summed = None
                for k in range(plane):
                    same = refs[k][r, pl.ds(size, 1), :] == last[:1]
                    one = jnp.where(same, refs[k][r, pl.ds(0, size), :], 0.0)
                    summed = one if summed is None else summed + one
                out[r, pl.ds(0, size), :] = summed
                out[r, pl.ds(size, 8), :] = last

        (total_share,) = small_call(self.turns, total, [self.share], (self.place, *self.swapped))
        self.passed = []
        for step in range(1, self.planes):
            shift = -step * plane if self.reverse else step * plane
            moves = [(i, i + shift) for i in range(self.count) if 0 <= i + shift < self.count]
            self.passed.append(lax.ppermute(total_share, "seq", moves))

    def swap_back(self):
        plane, size, planes = self.plane, self.size, self.planes

        def results(at_ref, *refs):
            shares, passed, outs = refs[:plane], refs[plane : plane + planes - 1], refs[plane + planes - 1 :]
            z_at, at = at_ref[0], at_ref[1]
            for r in range(self.row_count):
                ids = [one[r, pl.ds(size, 8), :] for one in shares]
                far_ids = [one[r, pl.ds(size, 8), :] for one in passed]
                there = [
                    (z_at + step < planes) if self.reverse else (z_at >= step) for step in range(1, planes)
                ]
                for k in range(plane):
                    target = at ^ k
                    near = jnp.where(there[0], far_ids[0], -1.0) if planes > 1 else jnp.full_like(ids[0], -1.0)
                    beside = target + 1 if self.reverse else target - 1
                    for j in range(plane):
                        near = jnp.where((at ^ j) == beside, ids[j], near)
                    summed = jnp.zeros((size, 128), F32)
                    for j in range(plane):
                        before = (at ^ j) > target if self.reverse else (at ^ j) < target
                        same = before & (ids[j][:1] == near[:1])
                        summed = summed + jnp.where(same, shares[j][r, pl.ds(0, size), :], 0.0)
                    for one, far, is_there in zip(passed, far_ids, there):
                        same = is_there & (far[:1] == near[:1])
                        summed = summed + jnp.where(same, one[r, pl.ds(0, size), :], 0.0)
                    outs[k][r, pl.ds(0, size), :] = summed
                    outs[k][r, pl.ds(size, 8), :] = near

        back = small_call(
            self.turns, results, [self.share] * plane, (self.place, *self.swapped, *self.passed)
        )
        self.back = self.swap(back)

    def join(self):
        plane, size = self.plane, self.size

        def join(at_ref, *refs):
            out, near = refs[plane:]
            for k in range(plane):
                begin = pl.multiple_of((at_ref[1] ^ k) * size, size)
                out[:, pl.ds(begin, size), :] = refs[k][:, pl.ds(0, size), :]
            near[...] = refs[0][:, pl.ds(size, 8), :]

        dims = (self.row_count, size * plane, 128)
        return small_call(
            self.turns, join, [shape(dims, F32), shape((self.row_count, 8, 128), F32)], (self.place, *self.back)
        )


class Scan:
    def __init__(self, turns, payload, reverse):
        self.turns = turns
        self.reverse = reverse
        self.count = lax.axis_size("seq")
        self.bits = self.count.bit_length() - 1
        self.position = lax.axis_index("seq")
        self.payload = payload
        self.result = None
        self.at = 0

    def send(self):
        flip = 1 << self.at
        self.got = lax.ppermute(self.payload, "seq", [(i, i ^ flip) for i in range(self.count)])

    def take(self):
        row_count, height, lanes = self.payload.shape
        depth = height - 16
        bit = ((self.position >> self.at) & 1).astype(jnp.int32).reshape(1)
        first = self.at == 0
        self.at += 1
        last = self.at == self.bits

        def add(bit_ref, own_ref, got_ref, *refs):
            earlier = bit_ref[0] == (0 if self.reverse else 1)
            outs = refs if first else refs[1:]
            ids = pl.ds(depth, 8)
            states = pl.ds(0, depth)
            sums = pl.ds(depth + 8, 8)
            for r in range(row_count):
                own_id, got_id = own_ref[r, ids, :], got_ref[r, ids, :]
                got = got_ref[r, states, :]
                near = jnp.full_like(own_id, -1.0) if first else refs[0][r, ids, :]
                near = jnp.where(earlier & (near < 0.0), got_id, near)
                outs[0][r, ids, :] = near
                for out in outs:
                    out[r, sums, :] = own_ref[r, sums, :] + got_ref[r, sums, :]
                use = earlier & (near[:1] == got_id[:1])
                kept = jnp.where(use, got, 0.0)
                outs[0][r, states, :] = kept if first else refs[0][r, states, :] + kept
                if not last:
                    same = own_id[:1] == got_id[:1]
                    outs[1][r, states, :] = jnp.where(same | earlier, own_ref[r, states, :], 0.0) + jnp.where(
                        same | jnp.logical_not(earlier), got, 0.0
                    )
                    outs[1][r, ids, :] = jnp.where(earlier, own_id, got_id)

        like = shape(self.payload.shape, F32)
        held = () if first else (self.result,)
        outs = small_call(
            self.turns, add, [like] * (1 if last else 2), (bit, self.payload, self.got, *held)
        )
        self.result = outs[0]
        if not last:
            self.payload = outs[1]


def softplus(v):
    return jnp.maximum(v, 0.0) + jnp.log1p(jnp.exp(-jnp.abs(v)))


def sigmoid(v):
    return 1.0 / (1.0 + jnp.exp(-v))


def sigmoid_of_softplus(s):
    return jnp.where(s < 0.01, s * (1.0 - s * (0.5 - s * (1.0 / 6.0))), 1.0 - jnp.exp(-s))


def mean_square(v):
    return jnp.mean(v * v, axis=-1, keepdims=True)


def head_ones():
    a = lax.broadcasted_iota(jnp.int32, (GROUP, GROUP), 0) >> 6
    b = lax.broadcasted_iota(jnp.int32, (GROUP, GROUP), 1) >> 6
    return jnp.where(a == b, 1.0 / HEAD_DIM, 0.0).astype(BF16)


def head_mean(v, ones):
    high = v.astype(BF16)
    low = (v - high.astype(F32)).astype(BF16)
    return dot(high, ones) + dot(low, ones)


def one_head(block, h):
    lanes = lax.broadcasted_iota(jnp.int32, (1, GROUP), 1) >> 6
    return jnp.where(lanes == h, block, jnp.zeros_like(block))


def pack_state(full):
    left = lax.broadcasted_iota(jnp.int32, (HEAD_DIM, 128), 1) < HEAD_DIM
    pairs = []
    for p in range(2):
        block = full[128 * p : 128 * p + 128, 128 * p : 128 * p + 128]
        pairs.append(jnp.where(left, block[:HEAD_DIM], block[HEAD_DIM:]))
    return jnp.concatenate(pairs, axis=0)


def unpack_state(packed):
    left = lax.broadcasted_iota(jnp.int32, (HEAD_DIM, 128), 1) < HEAD_DIM
    none = jnp.zeros((128, 128), F32)
    rows = []
    for p in range(2):
        block = packed[HEAD_DIM * p : HEAD_DIM * p + HEAD_DIM]
        square = jnp.concatenate([jnp.where(left, block, 0.0), jnp.where(left, 0.0, block)], axis=0)
        rows.append(jnp.concatenate([square, none] if p == 0 else [none, square], axis=1))
    return jnp.concatenate(rows, axis=0).astype(BF16)


def full_spec(dims, buffers=1):
    return pl.BlockSpec(dims, lambda *_: (0,) * len(dims), pipeline_mode=pl.Buffered(buffers))


def whole_out(dims):
    return pl.BlockSpec(dims, lambda *_: (0,) * len(dims))


def column_spec(tokens, tile, begin=0):
    return pl.BlockSpec((tokens, tile), lambda j, *_: (0, j + begin))


def row_spec(tile, width):
    return pl.BlockSpec((tile, width), lambda i, *_: (i, 0))


SMEM = pl.BlockSpec(memory_space=pltpu.SMEM)


def project_keys(turns, inputs, ids_col, last_ids, w_key, w_value, row_count):
    tokens, width = inputs.shape
    block = tokens // row_count

    def kernel(last_ref, x_ref, id_ref, wk_ref, wv_ref, xn_ref, k_ref, v_ref, s_ref):
        @pl.when(pl.program_id(0) == 0)
        def _():
            for i in range(tokens // TILE):
                x = x_ref[pl.ds(i * TILE, TILE), :].astype(F32)
                xn_ref[pl.ds(i * TILE, TILE), :] = (x * lax.rsqrt(mean_square(x) + EPSILON)).astype(BF16)

        xn = xn_ref[...]
        keys = softplus(dot(xn, wk_ref[...])).astype(BF16)
        values = dot(xn, wv_ref[...]).astype(BF16)
        k_ref[...] = keys
        v_ref[...] = values
        for r in range(row_count):
            at = slice(r * block, (r + 1) * block)
            kept = jnp.where(id_ref[at] == last_ref[r], keys[at], jnp.zeros((), BF16))
            s_ref[r] = pack_state(dot_tn(kept, values[at]))

    return turns.call(
        kernel,
        (width // GROUP,),
        [SMEM, full_spec((tokens, width)), full_spec((tokens, 1)), column_spec(width, GROUP), column_spec(width, GROUP)],
        [
            whole_out((tokens, width)),
            column_spec(tokens, GROUP),
            column_spec(tokens, GROUP),
            pl.BlockSpec((row_count, GROUP // 2, 128), lambda j: (0, j, 0)),
        ],
        [shape((tokens, width), BF16)] * 3 + [shape((row_count, width // 2, 128), F32)],
        us=9.5,
    )(last_ids, inputs, ids_col, w_key, w_value)


def block_mask(id_col, id_row, first, transposed):
    dims = (id_col.shape[0], id_row.shape[1])
    a = lax.broadcasted_iota(jnp.int32, dims, 0) + first
    b = lax.broadcasted_iota(jnp.int32, dims, 1)
    causal = b >= a if transposed else a >= b
    return jnp.where(causal & (id_col == id_row), 1.0, 0.0).astype(BF16)


def attend(turns, normed, keys, values, ids_col, ids_row, w_query, w_outgate, begin, end):
    tokens, width = normed.shape
    row_count, _, block = ids_row.shape

    def kernel(xn_ref, k_ref, v_ref, ic_ref, ir_ref, wq_ref, wg_ref, q_ref, g_ref, o_ref, mask_ref):
        @pl.when(pl.program_id(0) == 0)
        def _():
            for r in range(row_count):
                for i in range(block // TILE):
                    at = pl.ds(r * block + i * TILE, TILE)
                    mask_ref[at, :] = block_mask(ic_ref[at, :], ir_ref[r], i * TILE, False)

        xn = xn_ref[...]
        q_ref[...] = softplus(dot(xn, wq_ref[...])).astype(BF16)
        g_ref[...] = sigmoid(dot(xn, wg_ref[...])).astype(BF16)
        for r in range(row_count):
            base = r * block
            for i in range(block // TILE):
                rows = pl.ds(base + i * TILE, TILE)
                seen = (i + 1) * TILE
                q = q_ref[rows, :]
                mask = mask_ref[rows, pl.ds(0, seen)]
                total = None
                for h in range(4):
                    k = one_head(k_ref[pl.ds(base, seen), :], h)
                    v = one_head(v_ref[pl.ds(base, seen), :], h)
                    scores = dot_nt(q, k).astype(BF16) * mask
                    one = dot(scores, v)
                    total = one if total is None else total + one
                o_ref[rows, :] = total

    return turns.call(
        kernel,
        (end - begin,),
        [
            full_spec((tokens, width)),
            column_spec(tokens, GROUP, begin),
            column_spec(tokens, GROUP, begin),
            full_spec((tokens, 1)),
            full_spec((row_count, 1, block)),
            column_spec(width, GROUP, begin),
            column_spec(width, GROUP, begin),
        ],
        [column_spec(tokens, GROUP)] * 3,
        [shape((tokens, (end - begin) * GROUP), BF16)] * 2 + [shape((tokens, (end - begin) * GROUP), F32)],
        scratch=[pltpu.VMEM((tokens, block), BF16)],
        us=8.3,
    )(normed, keys, values, ids_col, ids_row, w_query, w_outgate)


def combine(turns, parts, inputs, carried, near_ids, ids_col, head_gain, w_output):
    tokens, width = inputs.shape
    row_count = carried.shape[0]
    block = tokens // row_count
    per_row = block // TILE
    number = len(parts)
    per_part = width // GROUP // number

    def kernel(*refs):
        (x_ref, c_ref, near_ref, id_ref, gain_ref, wo_ref) = refs[3 * number : 3 * number + 6]
        (at_ref, go_ref, h_ref, nm_ref) = refs[3 * number + 6 :]
        matched = id_ref[...] == near_ref[0, pl.ds(0, 1), pl.ds(0, 1)]
        ones = head_ones()
        for j in range(width // GROUP):
            q_ref, g_ref, in_ref = refs[3 * (j // per_part) : 3 * (j // per_part) + 3]
            own = pl.ds((j % per_part) * GROUP, GROUP)
            cols = pl.ds(j * GROUP, GROUP)
            state = unpack_state(c_ref[0, pl.ds(j * GROUP // 2, GROUP // 2), :])
            across = dot(q_ref[:, own], state)
            attended = in_ref[:, own] + jnp.where(matched, across, 0.0)
            at_ref[:, cols] = attended.astype(BF16)
            unit = attended * lax.rsqrt(head_mean(attended * attended, ones) + EPSILON)
            go_ref[:, cols] = (unit * gain_ref[:, cols] * g_ref[:, own].astype(F32)).astype(BF16)
        hidden = x_ref[...].astype(F32) + dot(go_ref[...], wo_ref[...])
        h_ref[...] = hidden
        nm_ref[...] = (hidden * lax.rsqrt(mean_square(hidden) + EPSILON)).astype(BF16)

    tile = row_spec(TILE, width)
    return turns.call(
        kernel,
        (tokens // TILE,),
        [row_spec(TILE, width // number)] * (3 * number)
        + [
            tile,
            pl.BlockSpec((1, width // 2, 128), lambda i: (i // per_row, 0, 0)),
            pl.BlockSpec((1, 8, 128), lambda i: (i // per_row, 0, 0)),
            row_spec(TILE, 1),
            full_spec((1, width)),
            full_spec((width, width)),
        ],
        [tile] * 4,
        [shape((tokens, width), BF16)] * 2 + [shape((tokens, width), F32), shape((tokens, width), BF16)],
        us=7.2,
    )(*[a for part in parts for a in part], inputs, carried, near_ids, ids_col, head_gain, w_output)


def back_product(turns, cotangent, w_down):
    tokens, width = cotangent.shape
    wide = w_down.shape[0]

    def kernel(c_ref, w_ref, o_ref):
        o_ref[...] = dot_nt(c_ref[...], w_ref[...]).astype(BF16)

    return turns.call(
        kernel,
        (wide // TILE,),
        [full_spec((tokens, width)), row_spec(TILE, width)],
        column_spec(tokens, TILE),
        shape((tokens, wide), BF16),
        us=8.5,
    )(cotangent, w_down)


def gate_up(turns, normed, w_gate, w_up, back):
    tokens, width = normed.shape
    wide = w_gate.shape[1]

    def kernel(n_ref, wg_ref, wu_ref, b_ref, p_ref, g_ref, u_ref):
        n = n_ref[...]
        gate = dot(n, wg_ref[...])
        up = dot(n, wu_ref[...])
        b = b_ref[...].astype(F32)
        p_ref[...] = (gate * up).astype(BF16)
        g_ref[...] = (b * up).astype(BF16)
        u_ref[...] = (b * gate).astype(BF16)

    tile = column_spec(tokens, TILE)
    return turns.call(
        kernel,
        (wide // TILE,),
        [full_spec((tokens, width)), column_spec(width, TILE), column_spec(width, TILE), tile],
        [tile] * 3,
        [shape((tokens, wide), BF16)] * 3,
        us=18,
    )(normed, w_gate, w_up, back)


def block_output(turns, hidden, product, w_down):
    tokens, width = hidden.shape
    wide = product.shape[1]

    def kernel(h_ref, p_ref, w_ref, o_ref):
        o_ref[...] = (h_ref[...] + dot(p_ref[...], w_ref[...])).astype(BF16)

    return turns.call(
        kernel,
        (tokens // TILE,),
        [row_spec(TILE, width), row_spec(TILE, wide), full_spec((wide, width))],
        row_spec(TILE, width),
        shape((tokens, width), BF16),
        us=9,
    )(hidden, product, w_down)


def norm_back(unit, scale, grad):
    return scale * (grad - unit * jnp.mean(grad * unit, axis=-1, keepdims=True))


def back_mid_heads(
    turns,
    back_gate,
    back_up,
    w_gate,
    w_up,
    cotangent,
    hidden,
    w_output,
    attended,
    parts,
    head_gain,
    first_ids,
    ids_col,
    row_count,
):
    tokens, width = cotangent.shape
    block = tokens // row_count
    per_row = block // TILE
    steps = back_gate.shape[1] // TILE
    number = len(parts)
    per_part = width // GROUP // number

    def kernel(first_ref, *refs):
        (bg_ref, bu_ref, wg_ref, wu_ref, c_ref, h_ref, wo_ref, at_ref, gain_ref, id_ref) = refs[:10]
        q_refs, g_refs = refs[10 : 10 + number], refs[10 + number : 10 + 2 * number]
        (bb_ref, bo_ref, ba_ref, s_ref, acc_ref) = refs[10 + 2 * number :]
        step = pl.program_id(0)

        @pl.when(step == 0)
        def _():
            acc_ref[...] = jnp.zeros_like(acc_ref)

        acc_ref[...] += dot_nt(bg_ref[...], wg_ref[...]) + dot_nt(bu_ref[...], wu_ref[...])

        @pl.when(step == steps - 1)
        def _():
            ones = head_ones()
            gains = [jnp.zeros((1, GROUP), F32)] * (width // GROUP)
            for r in range(row_count):
                sums = [None] * (width // GROUP)
                for i in range(per_row):
                    rows = pl.ds(r * block + i * TILE, TILE)
                    h = h_ref[rows, :]
                    scale = lax.rsqrt(mean_square(h) + EPSILON)
                    back = c_ref[rows, :].astype(F32) + norm_back(h * scale, scale, acc_ref[rows, :])
                    bb_ref[rows, :] = back.astype(BF16)
                    acc_ref[rows, :] = dot_nt(bb_ref[rows, :], wo_ref[...])
                    in_first = id_ref[rows, :] == first_ref[r]
                    for j in range(width // GROUP):
                        cols = pl.ds(j * GROUP, GROUP)
                        own = pl.ds((j % per_part) * GROUP, GROUP)
                        attended = at_ref[rows, cols].astype(F32)
                        scale_h = lax.rsqrt(head_mean(attended * attended, ones) + EPSILON)
                        unit = attended * scale_h
                        gate = g_refs[j // per_part][rows, own].astype(F32)
                        gain = gain_ref[:, cols]
                        gated = acc_ref[rows, cols] * gate
                        along = unit * gated
                        gains[j] = gains[j] + jnp.sum(along, axis=0, keepdims=True)
                        bo_ref[rows, cols] = (along * gain * (1.0 - gate)).astype(BF16)
                        back_unit = gated * gain
                        mean = head_mean(back_unit * unit, ones)
                        ba = (scale_h * (back_unit - unit * mean)).astype(BF16)
                        ba_ref[rows, cols] = ba
                        q = jnp.where(in_first, q_refs[j // per_part][rows, own], jnp.zeros((), BF16))
                        one = dot_tn(q, ba)
                        sums[j] = one if sums[j] is None else sums[j] + one
                for j in range(width // GROUP):
                    s_ref[r, pl.ds(j * GROUP // 2, GROUP // 2), :] = pack_state(sums[j])
                s_ref[r, pl.ds(width // 2, 8), :] = jnp.full((8, 128), first_ref[r])
            s_ref[:, pl.ds(width // 2 + 8, 8), :] = jnp.zeros((row_count, 8, 128), F32)
            for j in range(width // GROUP):
                for p in range(2):
                    s_ref[0, pl.ds(width // 2 + 8 + 2 * j + p, 1), :] = gains[j][:, 128 * p : 128 * p + 128]

    whole = full_spec((tokens, width))
    tile = column_spec(tokens, TILE)
    weights = column_spec(width, TILE)
    return turns.call(
        kernel,
        (steps,),
        [SMEM, tile, tile, weights, weights, whole, whole, full_spec((width, width)), whole, full_spec((1, width))]
        + [full_spec((tokens, 1))]
        + [full_spec((tokens, width // number))] * (2 * number),
        [whole_out((tokens, width))] * 3 + [whole_out((row_count, width // 2 + 16, 128))],
        [shape((tokens, width), BF16)] * 3 + [shape((row_count, width // 2 + 16, 128), F32)],
        scratch=[pltpu.VMEM((tokens, width), F32)],
        us=28,
    )(
        first_ids,
        back_gate,
        back_up,
        w_gate,
        w_up,
        cotangent,
        hidden,
        w_output,
        attended,
        head_gain,
        ids_col,
        *[part[0] for part in parts],
        *[part[1] for part in parts],
    )


def attend_back(turns, queries, keys, values, back_attended, carried, near_ids, ids_col, ids_row, begin):
    tokens, width = queries.shape
    row_count, _, block = ids_row.shape

    def kernel(near_ref, q_ref, k_ref, v_ref, a_ref, c_ref, ic_ref, ir_ref, bq_ref, bk_ref, bv_ref, mask_ref, flip_ref):
        @pl.when(pl.program_id(0) == 0)
        def _():
            for r in range(row_count):
                for i in range(block // TILE):
                    at = pl.ds(r * block + i * TILE, TILE)
                    mask_ref[at, :] = block_mask(ic_ref[at, :], ir_ref[r], i * TILE, False)
                    flip_ref[at, :] = block_mask(ic_ref[at, :], ir_ref[r], i * TILE, True)

        for r in range(row_count):
            base = r * block
            state = unpack_state(c_ref[r])
            for i in range(block // TILE):
                rows = pl.ds(base + i * TILE, TILE)
                seen = (i + 1) * TILE
                earlier = pl.ds(base, seen)
                later = pl.ds(base + i * TILE, block - i * TILE)
                a = a_ref[rows, :]
                q = q_ref[rows, :]
                k = k_ref[rows, :]
                v = v_ref[rows, :]
                matched = ic_ref[rows, :] == near_ref[r, pl.ds(0, 1), pl.ds(0, 1)]
                back_q = jnp.where(matched, dot_nt(a, state), 0.0)
                back_k = None
                back_v = None
                mask = mask_ref[rows, pl.ds(0, seen)]
                flip = flip_ref[rows, pl.ds(i * TILE, block - i * TILE)]
                for h in range(4):
                    grads = dot_nt(a, one_head(v_ref[earlier, :], h)).astype(BF16) * mask
                    back_q = back_q + dot(grads, one_head(k_ref[earlier, :], h))
                    q_h = one_head(q_ref[later, :], h)
                    a_h = one_head(a_ref[later, :], h)
                    scores_t = dot_nt(k, q_h).astype(BF16) * flip
                    grads_t = dot_nt(v, a_h).astype(BF16) * flip
                    one = dot(grads_t, q_h)
                    back_k = one if back_k is None else back_k + one
                    one = dot(scores_t, a_h)
                    back_v = one if back_v is None else back_v + one
                bq_ref[rows, :] = (back_q * sigmoid_of_softplus(q.astype(F32))).astype(BF16)
                bk_ref[rows, :] = back_k
                bv_ref[rows, :] = back_v

    tile = column_spec(tokens, GROUP)
    there = column_spec(tokens, GROUP, begin)
    return turns.call(
        kernel,
        (width // GROUP,),
        [full_spec((row_count, 8, 128)), tile, there, there, there]
        + [pl.BlockSpec((row_count, GROUP // 2, 128), lambda j: (0, j + begin, 0))]
        + [full_spec((tokens, 1)), full_spec((row_count, 1, block))],
        [tile] * 3,
        [shape((tokens, width), BF16)] + [shape((tokens, width), F32)] * 2,
        scratch=[pltpu.VMEM((tokens, block), BF16)] * 2,
        us=14,
    )(near_ids, queries, keys, values, back_attended, carried, ids_col, ids_row)


def finish_keys(turns, parts, keys, values, state_grad, ids_col):
    tokens, width = keys.shape
    row_count = state_grad.shape[0]
    block = tokens // row_count

    number = len(parts)
    per_part = width // GROUP // number

    def kernel(near_ref, k_ref, v_ref, s_ref, id_ref, *refs):
        ok_ref, ov_ref = refs[2 * number :]
        for i in range(number):

            @pl.when(pl.program_id(0) // per_part == i)
            def _(i=i):
                work(near_ref, k_ref, v_ref, s_ref, id_ref, refs[2 * i], refs[2 * i + 1], ok_ref, ov_ref)

    def work(near_ref, k_ref, v_ref, s_ref, id_ref, bk_ref, bv_ref, ok_ref, ov_ref):
        for r in range(row_count):
            rows = pl.ds(r * block, block)
            state = unpack_state(s_ref[r])
            uses = id_ref[rows, :] == near_ref[r, pl.ds(0, 1), pl.ds(0, 1)]
            k = k_ref[rows, :]
            back_k = bk_ref[rows, :] + jnp.where(uses, dot_nt(v_ref[rows, :], state), 0.0)
            ok_ref[rows, :] = (back_k * sigmoid_of_softplus(k.astype(F32))).astype(BF16)
            ov_ref[rows, :] = (bv_ref[rows, :] + jnp.where(uses, dot(k, state), 0.0)).astype(BF16)

    tile = column_spec(tokens, GROUP)

    def part(i):
        return pl.BlockSpec((tokens, GROUP), lambda j: (0, jnp.clip(j - i * per_part, 0, per_part - 1)))

    return turns.call(
        kernel,
        (width // GROUP,),
        [pl.BlockSpec((row_count, 8, 128), lambda j: (0, width // 16, 0)), tile, tile]
        + [pl.BlockSpec((row_count, GROUP // 2, 128), lambda j: (0, j, 0)), full_spec((tokens, 1))]
        + [part(i) for i in range(number) for _ in range(2)],
        [tile] * 2,
        [shape((tokens, width), BF16)] * 2,
        us=5,
    )(state_grad, keys, values, state_grad, ids_col, *[a for part in parts for a in part])


def input_gradient(turns, back_query_parts, grads, weights, inputs, back_branch):
    tokens, width = inputs.shape
    number = len(back_query_parts)
    narrow = width // number

    def kernel(*refs):
        q_refs, g_refs = refs[:number], refs[number : number + len(grads)]
        w_refs = refs[number + len(grads) : -3]
        x_ref, bb_ref, o_ref = refs[-3:]
        back = None
        for i, q_ref in enumerate(q_refs):
            one = dot_nt(q_ref[...], w_refs[0][:, pl.ds(i * narrow, narrow)])
            back = one if back is None else back + one
        for g_ref, w_ref in zip(g_refs, w_refs[1:]):
            back = back + dot_nt(g_ref[...], w_ref[...])
        x = x_ref[...].astype(F32)
        scale = lax.rsqrt(mean_square(x) + EPSILON)
        o_ref[...] = (bb_ref[...].astype(F32) + norm_back(x * scale, scale, back)).astype(BF16)

    tile = row_spec(TILE, width)
    return turns.call(
        kernel,
        (tokens // TILE,),
        [row_spec(TILE, narrow)] * number
        + [tile] * len(grads)
        + [full_spec((width, width))] * len(weights)
        + [tile] * 2,
        tile,
        shape((tokens, width), BF16),
        us=13,
    )(*back_query_parts, *grads, *weights, inputs, back_branch)


def local(
    inputs,
    doc_ids,
    w_query,
    w_key,
    w_value,
    w_outgate,
    w_output,
    w_gate,
    w_up,
    w_down,
    head_gain,
    cotangent,
):
    row_count, block_len, width = inputs.shape
    tokens = row_count * block_len
    x_first, y_first, z_order = orders(lax.axis_size("seq"))
    core = lax.axis_index("batch").astype(jnp.int32).reshape(1)
    x_flat = inputs.reshape(tokens, width)
    cot_flat = cotangent.reshape(tokens, width)
    gain = head_gain.reshape(1, width)
    ids = doc_ids.astype(F32)
    ids_col = ids.reshape(tokens, 1)
    ids_row = ids.reshape(row_count, 1, block_len)
    first_ids, last_ids = ids[:, 0], ids[:, -1]
    groups = width // GROUP

    turns = Turns()

    normed, keys, values, state = project_keys(turns, x_flat, ids_col, last_ids, w_key, w_value, row_count)
    before = Prefix(turns, state, doc_ids[:, -1], False)
    part_a = attend(turns, normed, keys, values, ids_col, ids_row, w_query, w_outgate, 0, groups // 2)
    before.pass_on()
    part_b = attend(turns, normed, keys, values, ids_col, ids_row, w_query, w_outgate, groups // 2, groups)
    before.swap_back()
    back = back_product(turns, cot_flat, w_down)
    carried, before_ids = before.join()
    parts = (part_a, part_b)
    attended, gated, hidden, normed_mid = combine(
        turns, parts, x_flat, carried, before_ids, ids_col, gain, w_output
    )
    product, back_gate, back_up = gate_up(turns, normed_mid, w_gate, w_up, back)

    down_sent, down_kept = grad_halves(turns, [(product, cot_flat)], core, 512, us=12)
    down_got = to_core(down_sent)
    gate_sent, gate_kept = grad_halves(turns, [(normed_mid, back_gate)], core, 1408, us=12)
    gate_got = to_core(gate_sent)
    up_sent, up_kept = grad_halves(turns, [(normed_mid, back_up)], core, 1408, us=12)
    up_got = to_core(up_sent)
    down = Scatter(turns, [down_kept, down_got], x_first)
    down.step()
    gate = Scatter(turns, [gate_kept, gate_got], y_first)
    gate.step()
    up = Scatter(turns, [up_kept, up_got], z_order + x_first)
    up.step()
    back_branch, back_outgate, back_attended, state_out = back_mid_heads(
        turns,
        back_gate,
        back_up,
        w_gate,
        w_up,
        cot_flat,
        hidden,
        w_output,
        attended,
        parts,
        gain,
        first_ids,
        ids_col,
        row_count,
    )
    scan = Scan(turns, state_out, True)
    scan.send()
    out_sent, out_kept = grad_halves(
        turns, [(gated, back_branch), (normed, back_outgate)], core, 512, us=10
    )
    out_got = to_core(out_sent)

    def within(i):
        return attend_back(
            turns, parts[i][0], keys, values, back_attended, carried, before_ids, ids_col, ids_row, i * groups // 2
        )

    back_a = within(0)
    scan.take()
    scan.send()
    outer = Scatter(turns, [out_kept, out_got], x_first + z_order)
    outer.step()
    back_b = within(1)
    scan.take()
    scan.send()
    down.step()
    q_sent, q_kept = grad_halves(turns, [(normed, back_a[0]), (normed, back_b[0])], core, 512, us=6)
    q_got = to_core(q_sent)
    scan.take()
    scan.send()
    up.step()
    gate.step()
    block_out = block_output(turns, hidden, product, w_down).reshape(inputs.shape)
    scan.take()
    back_key, back_value = finish_keys(
        turns, (back_a[1:], back_b[1:]), keys, values, scan.result, ids_col
    )
    query = Scatter(turns, [q_kept, q_got], y_first + z_order)
    query.step()
    kv_sent, kv_kept = grad_halves(turns, [(normed, back_key), (normed, back_value)], core, 512, True, us=10)
    kv_got = to_core(kv_sent)
    grad_down = down.finish_planes()
    outer.step()
    key = Scatter(turns, [kv_kept[:1], kv_got[:1]], x_first + z_order)
    key.step()
    value = Scatter(turns, [kv_kept[1:], kv_got[1:]], y_first + z_order)
    value.step()
    input_grad = input_gradient(
        turns,
        (back_a[0], back_b[0]),
        (back_key, back_value, back_outgate),
        (w_query, w_key, w_value, w_outgate),
        x_flat,
        back_branch,
    ).reshape(inputs.shape)
    up.step()
    grad_gate = gate.finish_planes()
    outer.step()
    query.step()
    key.step()
    value.step()
    up.step()
    outer.step()
    query.step()
    key.step()
    value.step()
    (grad_up,) = up.finish(w_gate.shape[1])
    grad_output, grad_outgate = outer.finish(width, width)
    query.step()
    key.step()
    value.step()
    (grad_query,) = query.finish(width)
    (grad_key,) = key.finish(width)
    (grad_value,) = value.finish(width)
    gain_sum = scan.result[0, -8:]
    gain_sum = (gain_sum + to_core([gain_sum])[0]).reshape(width)
    share = width // (2 * lax.axis_size("seq"))
    place = lax.axis_index("batch") * lax.axis_size("seq") + lax.axis_index("seq")
    grad_gain = lax.dynamic_slice_in_dim(gain_sum, place * share, share)
    return (
        block_out,
        input_grad,
        grad_query,
        grad_key,
        grad_value,
        grad_outgate,
        grad_output,
        grad_gate,
        grad_up,
        grad_down,
        grad_gain,
    )


def solution(mesh):
    rows = P("batch", "seq", None)
    scattered = P(("batch", "seq"), None)
    return jax.shard_map(
        local,
        mesh=mesh,
        in_specs=(rows, P("batch", "seq")) + (P(),) * 9 + (rows,),
        out_specs=(rows, rows) + (scattered,) * 8 + (P(("batch", "seq")),),
        check_vma=False,
    )
```

```python
import functools

import jax
import jax.numpy as jnp
from jax import lax
from jax.experimental import pallas as pl
from jax.experimental.pallas import tpu as pltpu
from jax.sharding import PartitionSpec as P

HEADS = 16
HEAD_DIM = 64
GROUP = 4 * HEAD_DIM
TILE = 256
EPSILON = 1e-06
F32 = jnp.float32
BF16 = jnp.bfloat16
VMEM_BYTES = 56 << 20
FLOPS_US = 1e11
STEPS = 2


def chip_grid(count):
    bits = count.bit_length() - 1
    z_bits = min(bits, 2)
    y_bits = (bits - z_bits + 1) // 2
    return z_bits, y_bits, bits - z_bits - y_bits


def orders(count):
    z_bits, y_bits, x_bits = chip_grid(count)
    z_axes = list(range(z_bits))[::-1]
    y_axes = list(range(z_bits, z_bits + y_bits))[::-1]
    x_axes = list(range(z_bits + y_bits, z_bits + y_bits + x_bits))[::-1]
    return x_axes + y_axes, y_axes + x_axes, z_axes


class Scatter:
    def __init__(self, turns, halves, order):
        self.turns = turns
        self.count = lax.axis_size("seq")
        self.bits = self.count.bit_length() - 1
        self.position = lax.axis_index("seq").astype(jnp.int32).reshape(1)
        self.rows = halves[0][0].shape[0] // self.count
        axes = tuple(range(self.bits))
        self.parts = [
            ([h.reshape((self.count, self.rows, h.shape[1])) for h in half], axes, 0) for half in halves
        ]
        self.width = sum(h.shape[1] for h in halves[0])
        self.order = list(order)
        self.done = ()

    def beside(self, others, order):
        for one in (self, *others):
            while one.order:
                one.step()
        for other in others:
            self.parts += [(held, axes, begin + self.width) for held, axes, begin in other.parts]
            self.width += other.width
        self.order = list(order)

    def total(self, flipped, widths=None):
        fixed = self.done if flipped is None else self.done + (flipped,)
        left = tuple(a for a in range(self.bits) if a not in fixed)
        bits, done = self.bits, self.done

        def block(axes, j, position):
            at = 0
            for a in axes:
                if a in left:
                    bit = (j >> (len(left) - 1 - left.index(a))) & 1
                else:
                    bit = (position[0] >> (bits - 1 - a)) & 1
                    if a == flipped:
                        bit = 1 - bit
                at = at * 2 + bit
            return at

        count = 1 << len(left)
        deep = max(1, count // STEPS)
        arrays, specs, places = [], [], []
        for held, axes, begin in self.parts:
            for array in held:
                wide = array.shape[2]
                for d in range(deep):
                    arrays.append(array)
                    specs.append(
                        pl.BlockSpec(
                            (1, self.rows, wide),
                            lambda j, position, axes=axes, d=d: (block(axes, j * deep + d, position), 0, 0),
                        )
                    )
                    places.append((d, begin, begin + wide))
                begin += wide
        final = widths is not None
        widths = widths or [self.width]

        def kernel(position_ref, *refs):
            ins, outs = refs[: len(arrays)], refs[len(arrays) :]
            edge = 0
            for out, wide in zip(outs, widths):
                covers = sorted({p[1:] for p in places if p[1] < edge + wide and p[2] > edge})
                smallest = [p for p in covers if not any(q != p and p[0] <= q[0] and q[1] <= p[1] for q in covers)]
                for d in range(deep):
                    for low, high in smallest:
                        low, high = max(low, edge), min(high, edge + wide)
                        one = None
                        for ref, (at, begin, stop) in zip(ins, places):
                            if at == d and begin <= low and high <= stop:
                                term = ref[0, :, pl.ds(low - begin, high - low)]
                                one = term if one is None else one + term
                        if final:
                            out[:, pl.ds(low - edge, high - low)] = one
                        else:
                            out[d, :, pl.ds(low - edge, high - low)] = one
                edge += wide

        if final:
            out_specs = [pl.BlockSpec((self.rows, w), lambda j, position: (0, 0)) for w in widths]
            out_shape = [shape((self.rows, w), F32) for w in widths]
        else:
            out_specs = [pl.BlockSpec((deep, self.rows, w), lambda j, position: (j, 0, 0)) for w in widths]
            out_shape = [shape((count, self.rows, w), F32) for w in widths]
        return self.turns.call(kernel, (count // deep,), specs, out_specs, out_shape, prefetch=1, us=2)(
            self.position, *arrays
        )

    def finish_planes(self):
        while self.order:
            self.step()
        (terms,) = self.total(None)
        return scatter_between_planes(terms.reshape(-1, terms.shape[2]))

    def step(self):
        axis = self.order.pop(0)
        (outgoing,) = self.total(axis)
        flip = 1 << (self.bits - 1 - axis)
        incoming = lax.ppermute(outgoing, "seq", [(i, i ^ flip) for i in range(self.count)])
        self.done = self.done + (axis,)
        left = tuple(a for a in range(self.bits) if a not in self.done)
        self.parts.append(([incoming], left, 0))

    def finish(self, *widths):
        while self.order:
            self.step()
        return self.total(None, list(widths))


def to_core(arrays):
    return [lax.ppermute(array, "batch", [(0, 1), (1, 0)]) for array in arrays]


class Turns:
    def __init__(self):
        self.last = ()

    def call(self, kernel, grid, in_specs, out_specs, out_shape, scratch=(), prefetch=0, us=10):
        given = len(in_specs) + prefetch
        waits = len(self.last)

        def body(*refs):
            kernel(*refs[:given], *refs[given + waits :])

        spec = pltpu.PrefetchScalarGridSpec(
            num_scalar_prefetch=prefetch,
            grid=grid,
            in_specs=list(in_specs) + [pl.BlockSpec(memory_space=pl.ANY)] * waits,
            out_specs=out_specs,
            scratch_shapes=scratch,
        )

        def run(*args):
            out = pl.pallas_call(
                body,
                grid_spec=spec,
                out_shape=out_shape,
                compiler_params=pltpu.CompilerParams(vmem_limit_bytes=VMEM_BYTES),
                cost_estimate=pl.CostEstimate(flops=int(us * FLOPS_US), bytes_accessed=0, transcendentals=0),
            )(*args, *self.last)
            self.last = (out[0] if isinstance(out, (list, tuple)) else out,)
            return out

        return run


def shape(dims, dtype):
    return jax.ShapeDtypeStruct(dims, dtype)


def dot(a, b):
    return lax.dot_general(a, b, (((1,), (0,)), ((), ())), preferred_element_type=F32)


def dot_nt(a, b):
    return lax.dot_general(a, b, (((1,), (1,)), ((), ())), preferred_element_type=F32)


def dot_tn(a, b):
    return lax.dot_general(a, b, (((0,), (0,)), ((), ())), preferred_element_type=F32)


def grad_halves(turns, pairs, core, tile, apart=False, us=10):
    tokens, width = pairs[0][0].shape
    wide = width // 2
    per = pairs[0][1].shape[1] // tile
    acts = []
    for one, _ in pairs:
        if not any(one is a for a in acts):
            acts.append(one)
    number, kinds = len(pairs), len(acts)
    which = [[one is a for a in acts].index(True) for one, _ in pairs]
    one_buffer = pl.Buffered(1)
    sent_half = pl.BlockSpec((tokens, wide), lambda j, s: (0, 1 - s[0]), pipeline_mode=one_buffer)
    kept_half = pl.BlockSpec((tokens, wide), lambda j, s: (0, s[0]), pipeline_mode=one_buffer)

    def kernel(core_ref, *refs):
        step = pl.program_id(0)
        outs = refs[2 * kinds + number :]
        for i in range(number):

            @pl.when((step >= i * per) & (step < (i + 1) * per))
            def _(i=i):
                grads = refs[2 * kinds + i][...]
                outs[i if apart else 0][...] = dot_tn(refs[2 * which[i]][...], grads)
                outs[number + i if apart else 1][...] = dot_tn(refs[2 * which[i] + 1][...], grads)

    def part(i):
        return pl.BlockSpec((tokens, tile), lambda j, s: (0, jnp.clip(j - i * per, 0, per - 1)))

    def out_part(i):
        if not apart:
            return pl.BlockSpec((wide, tile), lambda j, s: (0, j))
        return pl.BlockSpec((wide, tile), lambda j, s: (0, jnp.clip(j - i * per, 0, per - 1)))

    arrays = number if apart else 1
    cols = tile * per if apart else tile * per * number
    outs = turns.call(
        kernel,
        (per * number,),
        [sent_half, kept_half] * kinds + [part(i) for i in range(number)],
        [out_part(i) for i in range(arrays)] * 2,
        [shape((wide, cols), F32)] * (2 * arrays),
        prefetch=1,
        us=us,
    )(core, *[a for one in acts for a in (one, one)], *[g for _, g in pairs])
    return list(outs[:arrays]), list(outs[arrays:])


def scatter_between_planes(array):
    count = lax.axis_size("seq")
    planes = 1 << chip_grid(count)[0]
    plane = count // planes
    groups = [[k + plane * z for z in range(planes)] for k in range(plane)]
    return lax.psum_scatter(array, "seq", scatter_dimension=0, axis_index_groups=groups, tiled=True)


def small_call(turns, kernel, out_shape, args):
    def whole(array):
        return pl.BlockSpec(array.shape, lambda _: (0,) * len(array.shape))

    specs = [pl.BlockSpec(memory_space=pltpu.SMEM)] + [whole(a) for a in args[1:]]
    return turns.call(kernel, (1,), specs, [whole(o) for o in out_shape], out_shape, us=2)(*args)


class Prefix:
    def __init__(self, turns, state, edge_ids, reverse):
        self.turns = turns
        self.reverse = reverse
        self.count = lax.axis_size("seq")
        z_bits, y_bits, x_bits = chip_grid(self.count)
        self.planes = 1 << z_bits
        self.plane = plane = 1 << (y_bits + x_bits)
        position = lax.axis_index("seq")
        place = jnp.stack([position // plane, position % plane]).astype(jnp.int32)
        self.place = jnp.concatenate([place, edge_ids])
        row_count, depth, lanes = state.shape
        self.size = size = depth // plane
        self.row_count = row_count
        self.share = shape((row_count, size + 8, lanes), F32)

        def split(at_ref, s_ref, *outs):
            for k in range(plane):
                begin = pl.multiple_of((at_ref[1] ^ k) * size, size)
                outs[k][:, pl.ds(0, size), :] = s_ref[:, pl.ds(begin, size), :]
                for r in range(row_count):
                    outs[k][r, pl.ds(size, 8), :] = jnp.full((8, lanes), at_ref[2 + r].astype(F32))

        shares = small_call(turns, split, [self.share] * plane, (self.place, state))
        self.swapped = self.swap(shares)

    def swap(self, shares):
        plane = self.plane
        return [shares[0]] + [
            lax.ppermute(
                shares[k],
                "seq",
                [(i, (i // plane) * plane + ((i % plane) ^ k)) for i in range(self.count)],
            )
            for k in range(1, plane)
        ]

    def pass_on(self):
        plane, size = self.plane, self.size
        end = 0 if self.reverse else plane - 1

        def total(at_ref, *refs):
            out = refs[plane]
            for r in range(self.row_count):
                last = refs[0][r, pl.ds(size, 8), :]
                for k in range(1, plane):
                    last = jnp.where((at_ref[1] ^ k) == end, refs[k][r, pl.ds(size, 8), :], last)
                summed = None
                for k in range(plane):
                    same = refs[k][r, pl.ds(size, 1), :] == last[:1]
                    one = jnp.where(same, refs[k][r, pl.ds(0, size), :], 0.0)
                    summed = one if summed is None else summed + one
                out[r, pl.ds(0, size), :] = summed
                out[r, pl.ds(size, 8), :] = last

        (total_share,) = small_call(self.turns, total, [self.share], (self.place, *self.swapped))
        self.passed = []
        for step in range(1, self.planes):
            shift = -step * plane if self.reverse else step * plane
            moves = [(i, i + shift) for i in range(self.count) if 0 <= i + shift < self.count]
            self.passed.append(lax.ppermute(total_share, "seq", moves))

    def swap_back(self):
        plane, size, planes = self.plane, self.size, self.planes

        def results(at_ref, *refs):
            shares, passed, outs = refs[:plane], refs[plane : plane + planes - 1], refs[plane + planes - 1 :]
            z_at, at = at_ref[0], at_ref[1]
            for r in range(self.row_count):
                ids = [one[r, pl.ds(size, 8), :] for one in shares]
                far_ids = [one[r, pl.ds(size, 8), :] for one in passed]
                there = [
                    (z_at + step < planes) if self.reverse else (z_at >= step) for step in range(1, planes)
                ]
                for k in range(plane):
                    target = at ^ k
                    near = jnp.where(there[0], far_ids[0], -1.0) if planes > 1 else jnp.full_like(ids[0], -1.0)
                    beside = target + 1 if self.reverse else target - 1
                    for j in range(plane):
                        near = jnp.where((at ^ j) == beside, ids[j], near)
                    summed = jnp.zeros((size, 128), F32)
                    for j in range(plane):
                        before = (at ^ j) > target if self.reverse else (at ^ j) < target
                        same = before & (ids[j][:1] == near[:1])
                        summed = summed + jnp.where(same, shares[j][r, pl.ds(0, size), :], 0.0)
                    for one, far, is_there in zip(passed, far_ids, there):
                        same = is_there & (far[:1] == near[:1])
                        summed = summed + jnp.where(same, one[r, pl.ds(0, size), :], 0.0)
                    outs[k][r, pl.ds(0, size), :] = summed
                    outs[k][r, pl.ds(size, 8), :] = near

        back = small_call(
            self.turns, results, [self.share] * plane, (self.place, *self.swapped, *self.passed)
        )
        self.back = self.swap(back)

    def join(self):
        plane, size = self.plane, self.size

        def join(at_ref, *refs):
            out, near = refs[plane:]
            for k in range(plane):
                begin = pl.multiple_of((at_ref[1] ^ k) * size, size)
                out[:, pl.ds(begin, size), :] = refs[k][:, pl.ds(0, size), :]
            near[...] = refs[0][:, pl.ds(size, 8), :]

        dims = (self.row_count, size * plane, 128)
        return small_call(
            self.turns, join, [shape(dims, F32), shape((self.row_count, 8, 128), F32)], (self.place, *self.back)
        )


class Scan:
    def __init__(self, turns, payload, reverse):
        self.turns = turns
        self.reverse = reverse
        self.count = lax.axis_size("seq")
        self.bits = self.count.bit_length() - 1
        self.position = lax.axis_index("seq")
        self.payload = payload
        self.result = None
        self.at = 0

    def send(self):
        flip = 1 << self.at
        self.got = lax.ppermute(self.payload, "seq", [(i, i ^ flip) for i in range(self.count)])

    def take(self):
        row_count, height, lanes = self.payload.shape
        depth = height - 16
        bit = ((self.position >> self.at) & 1).astype(jnp.int32).reshape(1)
        first = self.at == 0
        self.at += 1
        last = self.at == self.bits

        def add(bit_ref, own_ref, got_ref, *refs):
            earlier = bit_ref[0] == (0 if self.reverse else 1)
            outs = refs if first else refs[1:]
            ids = pl.ds(depth, 8)
            states = pl.ds(0, depth)
            sums = pl.ds(depth + 8, 8)
            for r in range(row_count):
                own_id, got_id = own_ref[r, ids, :], got_ref[r, ids, :]
                got = got_ref[r, states, :]
                near = jnp.full_like(own_id, -1.0) if first else refs[0][r, ids, :]
                near = jnp.where(earlier & (near < 0.0), got_id, near)
                outs[0][r, ids, :] = near
                for out in outs:
                    out[r, sums, :] = own_ref[r, sums, :] + got_ref[r, sums, :]
                use = earlier & (near[:1] == got_id[:1])
                kept = jnp.where(use, got, 0.0)
                outs[0][r, states, :] = kept if first else refs[0][r, states, :] + kept
                if not last:
                    same = own_id[:1] == got_id[:1]
                    outs[1][r, states, :] = jnp.where(same | earlier, own_ref[r, states, :], 0.0) + jnp.where(
                        same | jnp.logical_not(earlier), got, 0.0
                    )
                    outs[1][r, ids, :] = jnp.where(earlier, own_id, got_id)

        like = shape(self.payload.shape, F32)
        held = () if first else (self.result,)
        outs = small_call(
            self.turns, add, [like] * (1 if last else 2), (bit, self.payload, self.got, *held)
        )
        self.result = outs[0]
        if not last:
            self.payload = outs[1]


def softplus(v):
    return jnp.maximum(v, 0.0) + jnp.log1p(jnp.exp(-jnp.abs(v)))


def sigmoid(v):
    return 1.0 / (1.0 + jnp.exp(-v))


def sigmoid_of_softplus(s):
    return jnp.where(s < 0.01, s * (1.0 - s * (0.5 - s * (1.0 / 6.0))), 1.0 - jnp.exp(-s))


def mean_square(v):
    return jnp.mean(v * v, axis=-1, keepdims=True)


def head_ones():
    a = lax.broadcasted_iota(jnp.int32, (GROUP, GROUP), 0) >> 6
    b = lax.broadcasted_iota(jnp.int32, (GROUP, GROUP), 1) >> 6
    return jnp.where(a == b, 1.0 / HEAD_DIM, 0.0).astype(BF16)


def head_mean(v, ones):
    high = v.astype(BF16)
    low = (v - high.astype(F32)).astype(BF16)
    return dot(high, ones) + dot(low, ones)


def one_head(block, h):
    lanes = lax.broadcasted_iota(jnp.int32, (1, GROUP), 1) >> 6
    return jnp.where(lanes == h, block, jnp.zeros_like(block))


def pack_state(full):
    left = lax.broadcasted_iota(jnp.int32, (HEAD_DIM, 128), 1) < HEAD_DIM
    pairs = []
    for p in range(2):
        block = full[128 * p : 128 * p + 128, 128 * p : 128 * p + 128]
        pairs.append(jnp.where(left, block[:HEAD_DIM], block[HEAD_DIM:]))
    return jnp.concatenate(pairs, axis=0)


def unpack_state(packed):
    left = lax.broadcasted_iota(jnp.int32, (HEAD_DIM, 128), 1) < HEAD_DIM
    none = jnp.zeros((128, 128), F32)
    rows = []
    for p in range(2):
        block = packed[HEAD_DIM * p : HEAD_DIM * p + HEAD_DIM]
        square = jnp.concatenate([jnp.where(left, block, 0.0), jnp.where(left, 0.0, block)], axis=0)
        rows.append(jnp.concatenate([square, none] if p == 0 else [none, square], axis=1))
    return jnp.concatenate(rows, axis=0).astype(BF16)


def full_spec(dims, buffers=1):
    return pl.BlockSpec(dims, lambda *_: (0,) * len(dims), pipeline_mode=pl.Buffered(buffers))


def whole_out(dims):
    return pl.BlockSpec(dims, lambda *_: (0,) * len(dims))


def column_spec(tokens, tile, begin=0):
    return pl.BlockSpec((tokens, tile), lambda j, *_: (0, j + begin))


def row_spec(tile, width):
    return pl.BlockSpec((tile, width), lambda i, *_: (i, 0))


SMEM = pl.BlockSpec(memory_space=pltpu.SMEM)


def project_keys(turns, inputs, ids_col, last_ids, w_key, w_value, row_count):
    tokens, width = inputs.shape
    block = tokens // row_count

    def kernel(last_ref, x_ref, id_ref, wk_ref, wv_ref, xn_ref, k_ref, v_ref, s_ref):
        @pl.when(pl.program_id(0) == 0)
        def _():
            for i in range(tokens // TILE):
                x = x_ref[pl.ds(i * TILE, TILE), :].astype(F32)
                xn_ref[pl.ds(i * TILE, TILE), :] = (x * lax.rsqrt(mean_square(x) + EPSILON)).astype(BF16)

        xn = xn_ref[...]
        keys = softplus(dot(xn, wk_ref[...])).astype(BF16)
        values = dot(xn, wv_ref[...]).astype(BF16)
        k_ref[...] = keys
        v_ref[...] = values
        for r in range(row_count):
            at = slice(r * block, (r + 1) * block)
            kept = jnp.where(id_ref[at] == last_ref[r], keys[at], jnp.zeros((), BF16))
            s_ref[r] = pack_state(dot_tn(kept, values[at]))

    return turns.call(
        kernel,
        (width // GROUP,),
        [SMEM, full_spec((tokens, width)), full_spec((tokens, 1)), column_spec(width, GROUP), column_spec(width, GROUP)],
        [
            whole_out((tokens, width)),
            column_spec(tokens, GROUP),
            column_spec(tokens, GROUP),
            pl.BlockSpec((row_count, GROUP // 2, 128), lambda j: (0, j, 0)),
        ],
        [shape((tokens, width), BF16)] * 3 + [shape((row_count, width // 2, 128), F32)],
        us=9.5,
    )(last_ids, inputs, ids_col, w_key, w_value)


def block_mask(id_col, id_row, first, transposed):
    dims = (id_col.shape[0], id_row.shape[1])
    a = lax.broadcasted_iota(jnp.int32, dims, 0) + first
    b = lax.broadcasted_iota(jnp.int32, dims, 1)
    causal = b >= a if transposed else a >= b
    return jnp.where(causal & (id_col == id_row), 1.0, 0.0).astype(BF16)


def attend(turns, normed, keys, values, ids_col, ids_row, w_query, w_outgate, begin, end):
    tokens, width = normed.shape
    row_count, _, block = ids_row.shape

    def kernel(xn_ref, k_ref, v_ref, ic_ref, ir_ref, wq_ref, wg_ref, q_ref, g_ref, o_ref, mask_ref):
        @pl.when(pl.program_id(0) == 0)
        def _():
            for r in range(row_count):
                for i in range(block // TILE):
                    at = pl.ds(r * block + i * TILE, TILE)
                    mask_ref[at, :] = block_mask(ic_ref[at, :], ir_ref[r], i * TILE, False)

        xn = xn_ref[...]
        q_ref[...] = softplus(dot(xn, wq_ref[...])).astype(BF16)
        g_ref[...] = sigmoid(dot(xn, wg_ref[...])).astype(BF16)
        for r in range(row_count):
            base = r * block
            for i in range(block // TILE):
                rows = pl.ds(base + i * TILE, TILE)
                seen = (i + 1) * TILE
                q = q_ref[rows, :]
                mask = mask_ref[rows, pl.ds(0, seen)]
                total = None
                for h in range(4):
                    k = one_head(k_ref[pl.ds(base, seen), :], h)
                    v = one_head(v_ref[pl.ds(base, seen), :], h)
                    scores = dot_nt(q, k).astype(BF16) * mask
                    one = dot(scores, v)
                    total = one if total is None else total + one
                o_ref[rows, :] = total

    return turns.call(
        kernel,
        (end - begin,),
        [
            full_spec((tokens, width)),
            column_spec(tokens, GROUP, begin),
            column_spec(tokens, GROUP, begin),
            full_spec((tokens, 1)),
            full_spec((row_count, 1, block)),
            column_spec(width, GROUP, begin),
            column_spec(width, GROUP, begin),
        ],
        [column_spec(tokens, GROUP)] * 3,
        [shape((tokens, (end - begin) * GROUP), BF16)] * 2 + [shape((tokens, (end - begin) * GROUP), F32)],
        scratch=[pltpu.VMEM((tokens, block), BF16)],
        us=8.3,
    )(normed, keys, values, ids_col, ids_row, w_query, w_outgate)


def combine(turns, parts, inputs, carried, near_ids, ids_col, head_gain, w_output):
    tokens, width = inputs.shape
    row_count = carried.shape[0]
    block = tokens // row_count
    per_row = block // TILE
    number = len(parts)
    per_part = width // GROUP // number

    def kernel(*refs):
        (x_ref, c_ref, near_ref, id_ref, gain_ref, wo_ref) = refs[3 * number : 3 * number + 6]
        (at_ref, go_ref, h_ref, nm_ref) = refs[3 * number + 6 :]
        matched = id_ref[...] == near_ref[0, pl.ds(0, 1), pl.ds(0, 1)]
        ones = head_ones()
        for j in range(width // GROUP):
            q_ref, g_ref, in_ref = refs[3 * (j // per_part) : 3 * (j // per_part) + 3]
            own = pl.ds((j % per_part) * GROUP, GROUP)
            cols = pl.ds(j * GROUP, GROUP)
            state = unpack_state(c_ref[0, pl.ds(j * GROUP // 2, GROUP // 2), :])
            across = dot(q_ref[:, own], state)
            attended = in_ref[:, own] + jnp.where(matched, across, 0.0)
            at_ref[:, cols] = attended.astype(BF16)
            unit = attended * lax.rsqrt(head_mean(attended * attended, ones) + EPSILON)
            go_ref[:, cols] = (unit * gain_ref[:, cols] * g_ref[:, own].astype(F32)).astype(BF16)
        hidden = x_ref[...].astype(F32) + dot(go_ref[...], wo_ref[...])
        h_ref[...] = hidden
        nm_ref[...] = (hidden * lax.rsqrt(mean_square(hidden) + EPSILON)).astype(BF16)

    tile = row_spec(TILE, width)
    return turns.call(
        kernel,
        (tokens // TILE,),
        [row_spec(TILE, width // number)] * (3 * number)
        + [
            tile,
            pl.BlockSpec((1, width // 2, 128), lambda i: (i // per_row, 0, 0)),
            pl.BlockSpec((1, 8, 128), lambda i: (i // per_row, 0, 0)),
            row_spec(TILE, 1),
            full_spec((1, width)),
            full_spec((width, width)),
        ],
        [tile] * 4,
        [shape((tokens, width), BF16)] * 2 + [shape((tokens, width), F32), shape((tokens, width), BF16)],
        us=7.2,
    )(*[a for part in parts for a in part], inputs, carried, near_ids, ids_col, head_gain, w_output)


def back_product(turns, cotangent, w_down):
    tokens, width = cotangent.shape
    wide = w_down.shape[0]
    tile = wide // 2

    def kernel(c_ref, w_ref, o_ref):
        o_ref[...] = dot_nt(c_ref[...], w_ref[...]).astype(BF16)

    return turns.call(
        kernel,
        (wide // tile,),
        [full_spec((tokens, width)), row_spec(tile, width)],
        column_spec(tokens, tile),
        shape((tokens, wide), BF16),
        us=8.5,
    )(cotangent, w_down)


def gate_up(turns, normed, w_gate, w_up, back):
    tokens, width = normed.shape
    wide = w_gate.shape[1]

    def kernel(n_ref, wg_ref, wu_ref, b_ref, p_ref, g_ref, u_ref):
        n = n_ref[...]
        gate = dot(n, wg_ref[...])
        up = dot(n, wu_ref[...])
        b = b_ref[...].astype(F32)
        p_ref[...] = (gate * up).astype(BF16)
        g_ref[...] = (b * up).astype(BF16)
        u_ref[...] = (b * gate).astype(BF16)

    tile = column_spec(tokens, TILE)
    return turns.call(
        kernel,
        (wide // TILE,),
        [full_spec((tokens, width)), column_spec(width, TILE), column_spec(width, TILE), tile],
        [tile] * 3,
        [shape((tokens, wide), BF16)] * 3,
        us=18,
    )(normed, w_gate, w_up, back)


def block_output(turns, hidden, product, w_down):
    tokens, width = hidden.shape
    wide = product.shape[1]

    def kernel(h_ref, p_ref, w_ref, o_ref):
        o_ref[...] = (h_ref[...] + dot(p_ref[...], w_ref[...])).astype(BF16)

    return turns.call(
        kernel,
        (tokens // TILE,),
        [row_spec(TILE, width), row_spec(TILE, wide), full_spec((wide, width))],
        row_spec(TILE, width),
        shape((tokens, width), BF16),
        us=9,
    )(hidden, product, w_down)


def norm_back(unit, scale, grad):
    return scale * (grad - unit * jnp.mean(grad * unit, axis=-1, keepdims=True))


def back_mid_heads(
    turns,
    back_gate,
    back_up,
    w_gate,
    w_up,
    cotangent,
    hidden,
    w_output,
    attended,
    parts,
    head_gain,
    first_ids,
    ids_col,
    row_count,
):
    tokens, width = cotangent.shape
    block = tokens // row_count
    per_row = block // TILE
    steps = back_gate.shape[1] // TILE
    number = len(parts)
    per_part = width // GROUP // number

    def kernel(first_ref, *refs):
        (bg_ref, bu_ref, wg_ref, wu_ref, c_ref, h_ref, wo_ref, at_ref, gain_ref, id_ref) = refs[:10]
        q_refs, g_refs = refs[10 : 10 + number], refs[10 + number : 10 + 2 * number]
        (bb_ref, bo_ref, ba_ref, s_ref, acc_ref) = refs[10 + 2 * number :]
        step = pl.program_id(0)

        @pl.when(step == 0)
        def _():
            acc_ref[...] = jnp.zeros_like(acc_ref)

        acc_ref[...] += dot_nt(bg_ref[...], wg_ref[...]) + dot_nt(bu_ref[...], wu_ref[...])

        @pl.when(step == steps - 1)
        def _():
            ones = head_ones()
            gains = [jnp.zeros((1, GROUP), F32)] * (width // GROUP)
            for r in range(row_count):
                sums = [None] * (width // GROUP)
                for i in range(per_row):
                    rows = pl.ds(r * block + i * TILE, TILE)
                    h = h_ref[rows, :]
                    scale = lax.rsqrt(mean_square(h) + EPSILON)
                    back = c_ref[rows, :].astype(F32) + norm_back(h * scale, scale, acc_ref[rows, :])
                    bb_ref[rows, :] = back.astype(BF16)
                    acc_ref[rows, :] = dot_nt(bb_ref[rows, :], wo_ref[...])
                    in_first = id_ref[rows, :] == first_ref[r]
                    for j in range(width // GROUP):
                        cols = pl.ds(j * GROUP, GROUP)
                        own = pl.ds((j % per_part) * GROUP, GROUP)
                        attended = at_ref[rows, cols].astype(F32)
                        scale_h = lax.rsqrt(head_mean(attended * attended, ones) + EPSILON)
                        unit = attended * scale_h
                        gate = g_refs[j // per_part][rows, own].astype(F32)
                        gain = gain_ref[:, cols]
                        gated = acc_ref[rows, cols] * gate
                        along = unit * gated
                        gains[j] = gains[j] + jnp.sum(along, axis=0, keepdims=True)
                        bo_ref[rows, cols] = (along * gain * (1.0 - gate)).astype(BF16)
                        back_unit = gated * gain
                        mean = head_mean(back_unit * unit, ones)
                        ba = (scale_h * (back_unit - unit * mean)).astype(BF16)
                        ba_ref[rows, cols] = ba
                        q = jnp.where(in_first, q_refs[j // per_part][rows, own], jnp.zeros((), BF16))
                        one = dot_tn(q, ba)
                        sums[j] = one if sums[j] is None else sums[j] + one
                for j in range(width // GROUP):
                    s_ref[r, pl.ds(j * GROUP // 2, GROUP // 2), :] = pack_state(sums[j])
                s_ref[r, pl.ds(width // 2, 8), :] = jnp.full((8, 128), first_ref[r])
            s_ref[:, pl.ds(width // 2 + 8, 8), :] = jnp.zeros((row_count, 8, 128), F32)
            for j in range(width // GROUP):
                for p in range(2):
                    s_ref[0, pl.ds(width // 2 + 8 + 2 * j + p, 1), :] = gains[j][:, 128 * p : 128 * p + 128]

    whole = full_spec((tokens, width))
    tile = column_spec(tokens, TILE)
    weights = column_spec(width, TILE)
    return turns.call(
        kernel,
        (steps,),
        [SMEM, tile, tile, weights, weights, whole, whole, full_spec((width, width)), whole, full_spec((1, width))]
        + [full_spec((tokens, 1))]
        + [full_spec((tokens, width // number))] * (2 * number),
        [whole_out((tokens, width))] * 3 + [whole_out((row_count, width // 2 + 16, 128))],
        [shape((tokens, width), BF16)] * 3 + [shape((row_count, width // 2 + 16, 128), F32)],
        scratch=[pltpu.VMEM((tokens, width), F32)],
        us=28,
    )(
        first_ids,
        back_gate,
        back_up,
        w_gate,
        w_up,
        cotangent,
        hidden,
        w_output,
        attended,
        head_gain,
        ids_col,
        *[part[0] for part in parts],
        *[part[1] for part in parts],
    )


def attend_back(turns, queries, keys, values, back_attended, carried, near_ids, ids_col, ids_row, begin):
    tokens, width = queries.shape
    row_count, _, block = ids_row.shape

    def kernel(near_ref, q_ref, k_ref, v_ref, a_ref, c_ref, ic_ref, ir_ref, bq_ref, bk_ref, bv_ref, mask_ref, flip_ref):
        @pl.when(pl.program_id(0) == 0)
        def _():
            for r in range(row_count):
                for i in range(block // TILE):
                    at = pl.ds(r * block + i * TILE, TILE)
                    mask_ref[at, :] = block_mask(ic_ref[at, :], ir_ref[r], i * TILE, False)
                    flip_ref[at, :] = block_mask(ic_ref[at, :], ir_ref[r], i * TILE, True)

        for r in range(row_count):
            base = r * block
            state = unpack_state(c_ref[r])
            for i in range(block // TILE):
                rows = pl.ds(base + i * TILE, TILE)
                seen = (i + 1) * TILE
                earlier = pl.ds(base, seen)
                later = pl.ds(base + i * TILE, block - i * TILE)
                a = a_ref[rows, :]
                q = q_ref[rows, :]
                k = k_ref[rows, :]
                v = v_ref[rows, :]
                matched = ic_ref[rows, :] == near_ref[r, pl.ds(0, 1), pl.ds(0, 1)]
                back_q = jnp.where(matched, dot_nt(a, state), 0.0)
                back_k = None
                back_v = None
                mask = mask_ref[rows, pl.ds(0, seen)]
                flip = flip_ref[rows, pl.ds(i * TILE, block - i * TILE)]
                for h in range(4):
                    grads = dot_nt(a, one_head(v_ref[earlier, :], h)).astype(BF16) * mask
                    back_q = back_q + dot(grads, one_head(k_ref[earlier, :], h))
                    q_h = one_head(q_ref[later, :], h)
                    a_h = one_head(a_ref[later, :], h)
                    scores_t = dot_nt(k, q_h).astype(BF16) * flip
                    grads_t = dot_nt(v, a_h).astype(BF16) * flip
                    one = dot(grads_t, q_h)
                    back_k = one if back_k is None else back_k + one
                    one = dot(scores_t, a_h)
                    back_v = one if back_v is None else back_v + one
                bq_ref[rows, :] = (back_q * sigmoid_of_softplus(q.astype(F32))).astype(BF16)
                bk_ref[rows, :] = back_k
                bv_ref[rows, :] = back_v

    tile = column_spec(tokens, GROUP)
    there = column_spec(tokens, GROUP, begin)
    return turns.call(
        kernel,
        (width // GROUP,),
        [full_spec((row_count, 8, 128)), tile, there, there, there]
        + [pl.BlockSpec((row_count, GROUP // 2, 128), lambda j: (0, j + begin, 0))]
        + [full_spec((tokens, 1)), full_spec((row_count, 1, block))],
        [tile] * 3,
        [shape((tokens, width), BF16)] + [shape((tokens, width), F32)] * 2,
        scratch=[pltpu.VMEM((tokens, block), BF16)] * 2,
        us=14,
    )(near_ids, queries, keys, values, back_attended, carried, ids_col, ids_row)


def finish_keys(turns, parts, keys, values, state_grad, ids_col):
    tokens, width = keys.shape
    row_count = state_grad.shape[0]
    block = tokens // row_count

    number = len(parts)
    per_part = width // GROUP // number

    def kernel(near_ref, k_ref, v_ref, s_ref, id_ref, *refs):
        ok_ref, ov_ref = refs[2 * number :]
        for i in range(number):

            @pl.when(pl.program_id(0) // per_part == i)
            def _(i=i):
                work(near_ref, k_ref, v_ref, s_ref, id_ref, refs[2 * i], refs[2 * i + 1], ok_ref, ov_ref)

    def work(near_ref, k_ref, v_ref, s_ref, id_ref, bk_ref, bv_ref, ok_ref, ov_ref):
        for r in range(row_count):
            rows = pl.ds(r * block, block)
            state = unpack_state(s_ref[r])
            uses = id_ref[rows, :] == near_ref[r, pl.ds(0, 1), pl.ds(0, 1)]
            k = k_ref[rows, :]
            back_k = bk_ref[rows, :] + jnp.where(uses, dot_nt(v_ref[rows, :], state), 0.0)
            ok_ref[rows, :] = (back_k * sigmoid_of_softplus(k.astype(F32))).astype(BF16)
            ov_ref[rows, :] = (bv_ref[rows, :] + jnp.where(uses, dot(k, state), 0.0)).astype(BF16)

    tile = column_spec(tokens, GROUP)

    def part(i):
        return pl.BlockSpec((tokens, GROUP), lambda j: (0, jnp.clip(j - i * per_part, 0, per_part - 1)))

    return turns.call(
        kernel,
        (width // GROUP,),
        [pl.BlockSpec((row_count, 8, 128), lambda j: (0, width // 16, 0)), tile, tile]
        + [pl.BlockSpec((row_count, GROUP // 2, 128), lambda j: (0, j, 0)), full_spec((tokens, 1))]
        + [part(i) for i in range(number) for _ in range(2)],
        [tile] * 2,
        [shape((tokens, width), BF16)] * 2,
        us=5,
    )(state_grad, keys, values, state_grad, ids_col, *[a for part in parts for a in part])


def input_gradient(turns, back_query_parts, grads, weights, inputs, back_branch):
    tokens, width = inputs.shape
    number = len(back_query_parts)
    narrow = width // number

    def kernel(*refs):
        q_refs, g_refs = refs[:number], refs[number : number + len(grads)]
        w_refs = refs[number + len(grads) : -3]
        x_ref, bb_ref, o_ref = refs[-3:]
        back = None
        for i, q_ref in enumerate(q_refs):
            one = dot_nt(q_ref[...], w_refs[0][:, pl.ds(i * narrow, narrow)])
            back = one if back is None else back + one
        for g_ref, w_ref in zip(g_refs, w_refs[1:]):
            back = back + dot_nt(g_ref[...], w_ref[...])
        x = x_ref[...].astype(F32)
        scale = lax.rsqrt(mean_square(x) + EPSILON)
        o_ref[...] = (bb_ref[...].astype(F32) + norm_back(x * scale, scale, back)).astype(BF16)

    tile = row_spec(TILE, width)
    return turns.call(
        kernel,
        (tokens // TILE,),
        [row_spec(TILE, narrow)] * number
        + [tile] * len(grads)
        + [full_spec((width, width))] * len(weights)
        + [tile] * 2,
        tile,
        shape((tokens, width), BF16),
        us=13,
    )(*back_query_parts, *grads, *weights, inputs, back_branch)


def local(
    inputs,
    doc_ids,
    w_query,
    w_key,
    w_value,
    w_outgate,
    w_output,
    w_gate,
    w_up,
    w_down,
    head_gain,
    cotangent,
):
    row_count, block_len, width = inputs.shape
    tokens = row_count * block_len
    x_first, y_first, z_order = orders(lax.axis_size("seq"))
    core = lax.axis_index("batch").astype(jnp.int32).reshape(1)
    x_flat = inputs.reshape(tokens, width)
    cot_flat = cotangent.reshape(tokens, width)
    gain = head_gain.reshape(1, width)
    ids = doc_ids.astype(F32)
    ids_col = ids.reshape(tokens, 1)
    ids_row = ids.reshape(row_count, 1, block_len)
    first_ids, last_ids = ids[:, 0], ids[:, -1]
    groups = width // GROUP

    turns = Turns()

    normed, keys, values, state = project_keys(turns, x_flat, ids_col, last_ids, w_key, w_value, row_count)
    before = Prefix(turns, state, doc_ids[:, -1], False)
    part_a = attend(turns, normed, keys, values, ids_col, ids_row, w_query, w_outgate, 0, groups // 2)
    before.pass_on()
    part_b = attend(turns, normed, keys, values, ids_col, ids_row, w_query, w_outgate, groups // 2, groups)
    before.swap_back()
    back = back_product(turns, cot_flat, w_down)
    carried, before_ids = before.join()
    parts = (part_a, part_b)
    attended, gated, hidden, normed_mid = combine(
        turns, parts, x_flat, carried, before_ids, ids_col, gain, w_output
    )
    product, back_gate, back_up = gate_up(turns, normed_mid, w_gate, w_up, back)

    down_sent, down_kept = grad_halves(turns, [(product, cot_flat)], core, 512, us=12)
    down_got = to_core(down_sent)
    gate_sent, gate_kept = grad_halves(turns, [(normed_mid, back_gate)], core, 1408, us=12)
    gate_got = to_core(gate_sent)
    up_sent, up_kept = grad_halves(turns, [(normed_mid, back_up)], core, 1408, us=12)
    up_got = to_core(up_sent)
    down = Scatter(turns, [down_kept, down_got], x_first)
    down.step()
    gate = Scatter(turns, [gate_kept, gate_got], y_first)
    gate.step()
    up = Scatter(turns, [up_kept, up_got], z_order + x_first)
    up.step()
    back_branch, back_outgate, back_attended, state_out = back_mid_heads(
        turns,
        back_gate,
        back_up,
        w_gate,
        w_up,
        cot_flat,
        hidden,
        w_output,
        attended,
        parts,
        gain,
        first_ids,
        ids_col,
        row_count,
    )
    scan = Scan(turns, state_out, True)
    scan.send()
    out_sent, out_kept = grad_halves(
        turns, [(gated, back_branch), (normed, back_outgate)], core, 512, us=10
    )
    out_got = to_core(out_sent)

    def within(i):
        return attend_back(
            turns, parts[i][0], keys, values, back_attended, carried, before_ids, ids_col, ids_row, i * groups // 2
        )

    back_a = within(0)
    scan.take()
    scan.send()
    outer = Scatter(turns, [out_kept, out_got], x_first + z_order)
    outer.step()
    back_b = within(1)
    scan.take()
    scan.send()
    down.step()
    q_sent, q_kept = grad_halves(turns, [(normed, back_a[0]), (normed, back_b[0])], core, 512, us=6)
    q_got = to_core(q_sent)
    scan.take()
    scan.send()
    up.step()
    gate.step()
    block_out = block_output(turns, hidden, product, w_down).reshape(inputs.shape)
    scan.take()
    back_key, back_value = finish_keys(
        turns, (back_a[1:], back_b[1:]), keys, values, scan.result, ids_col
    )
    query = Scatter(turns, [q_kept, q_got], y_first + z_order)
    query.step()
    kv_sent, kv_kept = grad_halves(turns, [(normed, back_key), (normed, back_value)], core, 512, True, us=10)
    kv_got = to_core(kv_sent)
    grad_down = down.finish_planes()
    outer.step()
    key = Scatter(turns, [kv_kept[:1], kv_got[:1]], x_first + z_order)
    key.step()
    value = Scatter(turns, [kv_kept[1:], kv_got[1:]], y_first + z_order)
    value.step()
    input_grad = input_gradient(
        turns,
        (back_a[0], back_b[0]),
        (back_key, back_value, back_outgate),
        (w_query, w_key, w_value, w_outgate),
        x_flat,
        back_branch,
    ).reshape(inputs.shape)
    up.step()
    grad_gate = gate.finish_planes()
    outer.step()
    query.step()
    key.step()
    value.step()
    up.step()
    outer.step()
    query.step()
    key.step()
    value.step()
    (grad_up,) = up.finish(w_gate.shape[1])
    grad_output, grad_outgate = outer.finish(width, width)
    query.step()
    key.step()
    value.step()
    (grad_query,) = query.finish(width)
    (grad_key,) = key.finish(width)
    (grad_value,) = value.finish(width)
    gain_sum = scan.result[0, -8:]
    gain_sum = (gain_sum + to_core([gain_sum])[0]).reshape(width)
    share = width // (2 * lax.axis_size("seq"))
    place = lax.axis_index("batch") * lax.axis_size("seq") + lax.axis_index("seq")
    grad_gain = lax.dynamic_slice_in_dim(gain_sum, place * share, share)
    return (
        block_out,
        input_grad,
        grad_query,
        grad_key,
        grad_value,
        grad_outgate,
        grad_output,
        grad_gate,
        grad_up,
        grad_down,
        grad_gain,
    )


def solution(mesh):
    rows = P("batch", "seq", None)
    scattered = P(("batch", "seq"), None)
    return jax.shard_map(
        local,
        mesh=mesh,
        in_specs=(rows, P("batch", "seq")) + (P(),) * 9 + (rows,),
        out_specs=(rows, rows) + (scattered,) * 8 + (P(("batch", "seq")),),
        check_vma=False,
    )
```
